32 devices in a mesh: elem: 8 (over y, x, core), band: 4 (over z).
Axes of the slice: x: 2, y: 2, z: 4, core: 2. Of those that a mesh axis runs over, the one named last changes fastest.
Arguments:
- orbitals: float32 [32, 160, 1024], P('elem', 'band'), may hold values from -6 to 6
- rotation: float32 [1024, 1024], P('band'), may hold values from -0.25 to 0.25
- counts: int32 [32], P('elem'), may hold values from 96 to 160, as said below
- hamiltonian: float32 [32, 7, 160, 160], P('elem'), may hold values from -0.1875 to 0.1875
- filter_center: float32 [1], replicated, may hold values from -0.5 to 0.5
- filter_width: float32 [1], replicated, may hold values from 1.5 to 2.5
Outputs:
- filtered: float32 [32, 160, 1024], P('elem', None, 'band')
The draws below stay inside these ranges and needn't reach their ends.
Inputs may be any that keep to these rules, and one draw needn't show every extreme that they name: `counts`: some element has exactly 96 and some exactly 160 basis functions.
All inputs are finite; a program needn't handle non-finite values.
Results may differ from the reference program's by a relative error of at most 0.0001.
Values sent between devices are 32-bit elements; how exact they have to be, the bound alone decides.
A program may use at most 64 MiB of HBM per device.

```python
import jax
import jax.numpy as jnp
from jax import lax

NB = 160
NBAND = 1024
GX = 4
GY = 8
CMIN = 96
GZ = 1
E = 32


def draw_counts(key, part):
    first, second, third = jax.random.split(jax.random.fold_in(key, 11), 3)
    values = jax.random.randint(first, (E,), CMIN, NB + 1, dtype=jnp.int32)
    high_spot = jax.random.randint(second, (), 0, E, dtype=jnp.int32)
    low_spot = (high_spot + 1 + jax.random.randint(third, (), 0, E - 1, dtype=jnp.int32)) % E
    values = values.at[high_spot].set(NB)
    values = values.at[low_spot].set(CMIN)
    return values


def raised(entries, stream_key, source, target, shards_of, factor):
    owner, partner = [(jnp.arange(entries.shape[axis_at]) // (entries.shape[axis_at] // shards_of)).reshape([-1 if axis == axis_at else 1 for axis in range(entries.ndim)]) for axis_at in (source, target)]
    chosen = jax.random.permutation(stream_key, shards_of)[partner]
    strong = (owner == chosen) | (owner == (partner + shards_of // 2) % shards_of)
    return jnp.where(strong, factor * entries, entries)


def levels(stream_key, extent, cuts, smallest, largest):
    gain, own = 1.0, jax.random.fold_in(stream_key, 6)
    for dim, parts in cuts:
        steps = jnp.exp(jax.random.uniform(jax.random.fold_in(own, dim), (parts,), jnp.float32, smallest / len(cuts), largest / len(cuts)))
        gain = gain * jnp.repeat(steps, extent[dim] // parts).reshape([-1 if axis == dim else 1 for axis in range(len(extent))])
    return gain


def bell_draw(stream_key, dims, scale, limit, pieces=(), kind=jnp.bfloat16):
    drawn = scale * jax.random.normal(stream_key, dims, jnp.float32)
    if pieces:
        drawn = drawn * levels(stream_key, dims, pieces, -0.22, 0.18)
    return jnp.clip(drawn, -limit, limit).astype(kind)


def noise_with(key, extent, spread, reach, pieces, heavy, kind=jnp.bfloat16):
    values = spread * jax.random.normal(key, extent, jnp.float32)
    if pieces:
        values = values * levels(key, extent, pieces, -0.22, 0.18)
    return jnp.clip(raised(values, jax.random.fold_in(key, 3), *heavy), -reach, reach).astype(kind)


def setup_inputs(seed: int = 0) -> dict:
    key_list = jax.random.split(jax.random.key(seed), 7)
    return {
        "orbitals": bell_draw(key_list[0], (E, NB, NBAND), 1.0, 6.0, ((0, 8), (1, 4)), jnp.float32),
        "rotation": noise_with(key_list[1], (NBAND, NBAND), NBAND ** -0.5, 0.25, ((0, 4),), (0, 1, 4, 2.0), jnp.float32),
        "counts": draw_counts(jax.random.fold_in(key_list[6], 71), 0),
        "hamiltonian": bell_draw(key_list[3], (E, 7, NB, NB), (7 * NB) ** -0.5, 0.1875, ((0, 8),), jnp.float32),
        "filter_center": jnp.clip(jax.random.uniform(key_list[4], (1,), jnp.float32, -0.5, 0.5), -0.5, 0.5),
        "filter_width": jnp.clip(jax.random.uniform(key_list[5], (1,), jnp.float32, 1.5, 2.5), 1.5, 2.5),
    }


def neighbour_fields(field):
    grid = field.reshape(GZ, GY, GX, NB, NBAND)
    zeros = jnp.zeros((1, GY, GX, NB, NBAND), jnp.float32)
    below = jnp.concatenate([zeros, grid[:-1]], axis=0)
    above = jnp.concatenate([grid[1:], zeros], axis=0)
    fields = [grid, jnp.roll(grid, 1, axis=2), jnp.roll(grid, -1, axis=2), jnp.roll(grid, 1, axis=1), jnp.roll(grid, -1, axis=1), below, above]
    return [f.reshape(E, NB, NBAND) for f in fields]


def apply_operator(field, hamiltonian, live):
    total = jnp.zeros((E, NB, NBAND), jnp.float32)
    for slot, other in enumerate(neighbour_fields(field)):
        total = total + jnp.einsum("erc,ecb->erb", hamiltonian[:, slot], other, precision=lax.Precision.HIGHEST)
    return jnp.where(live[:, :, None], total, jnp.float32(0.0))


def reference(orbitals, rotation, counts, hamiltonian, filter_center, filter_width):
    live = jnp.arange(NB, dtype=jnp.int32)[None, :] < counts[:, None]
    masked = jnp.where(live[:, :, None], orbitals, jnp.float32(0.0))
    start = jnp.einsum("eik,kb->eib", masked, rotation, precision=lax.Precision.HIGHEST)
    center = filter_center[0]
    width = filter_width[0]
    middle = (apply_operator(start, hamiltonian, live) - center * start) / width
    filtered = 2.0 * (apply_operator(middle, hamiltonian, live) - center * middle) / width - start
    return filtered
```

```python
import jax
import jax.numpy as jnp
from jax import lax
from jax.sharding import PartitionSpec as P

GY = 8


def neighbour_rows(field, stride, span, wraps):
    size = lax.axis_size("elem")
    behind, ahead = [], []
    for i in range(size):
        place = (i // stride) % span
        base = i - place * stride
        if wraps or place + 1 < span:
            behind.append((i, base + (place + 1) % span * stride))
        if wraps or place > 0:
            ahead.append((i, base + (place + span - 1) % span * stride))
    return lax.ppermute(field, "elem", behind), lax.ppermute(field, "elem", ahead)


def apply_operator(field, hamiltonian, live):
    layers = lax.axis_size("elem") // GY
    others = [field, jnp.roll(field, 1, axis=0), jnp.roll(field, -1, axis=0)]
    others += neighbour_rows(field, 1, GY, True)
    if layers > 1:
        others += neighbour_rows(field, GY, layers, False)
    total = jnp.zeros(field.shape, jnp.float32)
    for slot, other in enumerate(others):
        total = total + jnp.einsum(
            "erc,ecb->erb", hamiltonian[:, slot], other, precision=lax.Precision.HIGH
        )
    return jnp.where(live[:, :, None], total, jnp.float32(0.0))


def shards(orbitals, rotation, counts, hamiltonian, filter_center, filter_width):
    elements, rows_here, bands = orbitals.shape
    basis = hamiltonian.shape[2]
    whole_rotation = lax.all_gather(rotation, "band", axis=0, tiled=True)
    rotated = jnp.einsum(
        "eik,kb->eib", orbitals, whole_rotation, precision=lax.Precision.HIGH
    )
    start = lax.all_to_all(rotated, "band", split_axis=2, concat_axis=1, tiled=True)
    live = jnp.arange(basis, dtype=jnp.int32)[None, :] < counts[:, None]
    start = jnp.where(live[:, :, None], start, jnp.float32(0.0))
    center = filter_center[0]
    width = filter_width[0]
    middle = (apply_operator(start, hamiltonian, live) - center * start) / width
    return 2.0 * (apply_operator(middle, hamiltonian, live) - center * middle) / width - start


def solution(mesh):
    return jax.shard_map(
        shards,
        mesh=mesh,
        in_specs=(
            P("elem", "band", None),
            P("band", None),
            P("elem"),
            P("elem", None, None, None),
            P(),
            P(),
        ),
        out_specs=P("elem", None, "band"),
        check_vma=False,
    )
```

```python
import functools

import jax
import jax.numpy as jnp
from jax import lax
from jax.experimental import pallas as pl
from jax.experimental.pallas import tpu as pltpu
from jax.sharding import PartitionSpec as P

GY = 8


def neighbour_rows(field, stride, span, wraps):
    size = lax.axis_size("elem")
    behind, ahead = [], []
    for i in range(size):
        place = (i // stride) % span
        base = i - place * stride
        if wraps or place + 1 < span:
            behind.append((i, base + (place + 1) % span * stride))
        if wraps or place > 0:
            ahead.append((i, base + (place + span - 1) % span * stride))
    return lax.ppermute(field, "elem", behind), lax.ppermute(field, "elem", ahead)


def apply_operator(field, hamiltonian, live):
    layers = lax.axis_size("elem") // GY
    others = [field, jnp.roll(field, 1, axis=0), jnp.roll(field, -1, axis=0)]
    others += neighbour_rows(field, 1, GY, True)
    if layers > 1:
        others += neighbour_rows(field, GY, layers, False)
    total = jnp.zeros(field.shape, jnp.float32)
    for slot, other in enumerate(others):
        total = total + jnp.einsum(
            "erc,ecb->erb", hamiltonian[:, slot], other, precision=lax.Precision.HIGH
        )
    return jnp.where(live[:, :, None], total, jnp.float32(0.0))


def general_shards(orbitals, rotation, counts, hamiltonian, filter_center, filter_width):
    elements, rows_here, bands = orbitals.shape
    basis = hamiltonian.shape[2]
    whole_rotation = lax.all_gather(rotation, "band", axis=0, tiled=True)
    rotated = jnp.einsum(
        "eik,kb->eib", orbitals, whole_rotation, precision=lax.Precision.HIGH
    )
    start = lax.all_to_all(rotated, "band", split_axis=2, concat_axis=1, tiled=True)
    live = jnp.arange(basis, dtype=jnp.int32)[None, :] < counts[:, None]
    start = jnp.where(live[:, :, None], start, jnp.float32(0.0))
    center = filter_center[0]
    width = filter_width[0]
    middle = (apply_operator(start, hamiltonian, live) - center * start) / width
    return 2.0 * (apply_operator(middle, hamiltonian, live) - center * middle) / width - start


F32, BF16 = jnp.float32, jnp.bfloat16
PARTS = 2
SLOTS = 5


def split(x):
    high = x.astype(BF16)
    return high, (x - high.astype(F32)).astype(BF16)


def kernel(
    n, orb, rot, counts, center, width, ham, out,
    ham_v, ham_b, orb_b, rot_b, res, acc_r, start, start_lo, start_hi, mid, mid_lo, mid_hi,
    field, acc, ham_sem,
    up_s, dn_s, z_r, y_s, y_r, c_s, c_r, a_s, a_r, h_s, h_r,
):
    e, z = lax.axis_index("elem"), lax.axis_index("band")
    elements, basis = ham.shape[0], ham.shape[2]
    rows = basis // n
    depth = rot.shape[0]
    lanes = start.shape[3]
    share = depth // 4
    y, c = e // 4, e % 2
    ahead, behind = lax.rem(e + 1, 8), lax.rem(e + 7, 8)
    across, twin = lax.rem(e + 4, 8), e + 1 - 2 * c
    others = [lax.rem(z + j, n) for j in range(1, n)]

    def remote(src, dst, send, recv, elem, band):
        return pltpu.make_async_remote_copy(
            src_ref=src, dst_ref=dst, send_sem=send, recv_sem=recv,
            device_id=(elem, band), device_id_type=pl.DeviceIdType.MESH,
        )

    def block(ref, part, s, yy, cc):
        first = pl.multiple_of((yy * 2 + cc) * share, share)
        return ref.at[part, s, pl.ds(first, share)]

    def up(part, s):
        b = block(rot_b, part, s, y, c)
        return remote(b, b, up_s.at[part, s], z_r.at[part, s], e, z + 1)

    def down(part, s):
        b = block(rot_b, part, s, y, c)
        return remote(b, b, dn_s.at[part, s], z_r.at[part, s], e, z - 1)

    def over_y(part, s):
        b = block(rot_b, part, s, y, c)
        return remote(b, b, y_s.at[part, s], y_r.at[part, s], across, z)

    def over_core(part, s, far):
        yy = 1 - y if far else y
        b = block(rot_b, part, s, yy, c)
        return remote(b, b, c_s.at[part, s, far], c_r.at[part, s, far], twin, z)

    def got(dst, recv):
        remote(dst, dst, recv, recv, twin, z).wait_recv()

    def to_band(part, to):
        return remote(
            res.at[part, to],
            start.at[part, :, pl.ds(pl.multiple_of(z * rows, rows), rows)],
            a_s.at[part, to], a_r.at[part, z], e, to,
        )

    def rows_of(ref, part, s):
        return ref.at[part, :, pl.ds(pl.multiple_of(s * rows, rows), rows)]

    def halo(stage, part, s):
        own, lo, hi = ((start, start_lo, start_hi), (mid, mid_lo, mid_hi))[stage]
        b = rows_of(own, part, s)
        return (
            remote(b, rows_of(lo, part, s), h_s.at[stage, part, s, 0], h_r.at[stage, part, s, 0], ahead, z),
            remote(b, rows_of(hi, part, s), h_s.at[stage, part, s, 1], h_r.at[stage, part, s, 1], behind, z),
        )

    barrier = pltpu.get_barrier_semaphore()
    partners = [(ahead, z), (behind, z), (across, z)] + [(e, other) for other in others]
    for elem, band in partners:
        pl.semaphore_signal(barrier, inc=1, device_id=(elem, band), device_id_type=pl.DeviceIdType.MESH)
    ham_copy = pltpu.make_async_copy(ham.at[:, pl.ds(0, SLOTS)], ham_v, ham_sem)
    ham_copy.start()
    for part in range(PARTS):
        for b in range(n):
            rot_b[part, z, :, b * lanes:(b + 1) * lanes] = rot[:, (b * PARTS + part) * lanes:(b * PARTS + part + 1) * lanes]
    pl.semaphore_wait(barrier, len(partners))

    def send_own(part):
        @pl.when(z < n - 1)
        def _():
            up(part, z).start()

        @pl.when(z > 0)
        def _():
            down(part, z).start()

    def relay(part, d):
        @pl.when(z >= d)
        def _():
            s = z - d
            got(block(rot_b, part, s, y, c), z_r.at[part, s])

            @pl.when(z < n - 1)
            def _():
                up(part, s).start()

            over_y(part, s).start()
            over_core(part, s, 0).start()

        @pl.when(z + d < n)
        def _():
            s = z + d
            got(block(rot_b, part, s, y, c), z_r.at[part, s])

            @pl.when(z > 0)
            def _():
                down(part, s).start()

            over_y(part, s).start()
            over_core(part, s, 0).start()

    def relay_y(part):
        for s in others:
            got(block(rot_b, part, s, 1 - y, c), y_r.at[part, s])
            over_core(part, s, 1).start()

    def rotate(part, s, first):
        columns = pl.ds(pl.multiple_of(s * depth, depth), depth)
        high, low = split(rot_b[part, s])
        both = jnp.dot(orb_b[:, columns], high, preferred_element_type=F32)
        cross = jnp.dot(orb_b[:elements * rows, columns], low, preferred_element_type=F32)
        total = both[:elements * rows] + both[elements * rows:] + cross
        acc_r[part] = total if first else acc_r[part] + total

    def rotated(part):
        for s in others:
            for far in range(2):
                got(block(rot_b, part, s, 1 - y if far else y, 1 - c), c_r.at[part, s, far])
            rotate(part, s, False)
        for i in range(elements):
            place = lax.broadcasted_iota(jnp.int32, (rows, lanes), 0) + z * rows
            alive = place < counts[i]
            for b in range(n):
                piece = acc_r[part, i * rows:(i + 1) * rows, b * lanes:(b + 1) * lanes]
                res[part, b, i] = jnp.where(alive, piece, F32(0.0))
        for to in others:
            to_band(part, to).start()
        start[part, :, pl.ds(pl.multiple_of(z * rows, rows), rows)] = res[part, z]
        for copy in halo(0, part, z):
            copy.start()

    def spread(part):
        for s in others:
            got(rows_of(start, part, s), a_r.at[part, s])
            for copy in halo(0, part, s):
                copy.start()

    def load(k, ref, part):
        for i in range(elements):
            high, low = split(ref[part, i])
            field[k, i, :, :lanes] = high
            field[k, i, :, lanes:] = low

    def fold(r):
        return (r[:basis, :lanes] + r[:basis, lanes:]) + (r[basis:, :lanes] + r[basis:, lanes:])

    def local_slots(ref, part):
        load(0, ref, part)

        def body(i, carry):
            r = jnp.dot(ham_b[i, 0], field[0, i], preferred_element_type=F32)
            r += jnp.dot(ham_b[i, 1], field[0, lax.rem(i + elements - 1, elements)], preferred_element_type=F32)
            r += jnp.dot(ham_b[i, 2], field[0, lax.rem(i + 1, elements)], preferred_element_type=F32)
            acc[part, i] = fold(r)
            return carry

        lax.fori_loop(0, elements, body, 0)

    def halo_slots(stage, part, done):
        lo, hi = ((start_lo, start_hi), (mid_lo, mid_hi))[stage]
        for s in range(n):
            got(rows_of(lo, part, s), h_r.at[stage, part, s, 0])
            got(rows_of(hi, part, s), h_r.at[stage, part, s, 1])
        load(1, lo, part)
        load(2, hi, part)

        def body(i, carry):
            r = jnp.dot(ham_b[i, 3], field[1, i], preferred_element_type=F32)
            r += jnp.dot(ham_b[i, 4], field[2, i], preferred_element_type=F32)
            done(i, acc[part, i] + fold(r))
            return carry

        lax.fori_loop(0, elements, body, 0)

    send_own(0)
    high, low = split(orb[...])
    orb_b[:elements * rows] = high
    orb_b[elements * rows:] = low
    relay(0, 1)
    send_own(1)
    rotate(0, z, True)
    relay(0, 2)
    relay(0, 3)
    relay(1, 1)
    relay_y(0)
    relay(1, 2)
    rotated(0)
    relay(1, 3)
    relay_y(1)
    rotate(1, z, True)
    rotated(1)
    spread(0)

    ham_copy.wait()

    def prepare(i, carry):
        square = (basis, basis)
        place = lax.broadcasted_iota(jnp.int32, square, 0)
        scale = jnp.where(place < counts[i], 1.0 / jnp.full(square, width[0], F32), F32(0.0))
        diagonal = jnp.where(place == lax.broadcasted_iota(jnp.int32, square, 1), center[0], F32(0.0))
        for slot in range(SLOTS):
            entries = ham_v[i, slot]
            if slot == 0:
                entries = entries - diagonal
            high, low = split(entries * scale)
            ham_b[i, slot, :basis] = high
            ham_b[i, slot, basis:] = low
        return carry

    lax.fori_loop(0, elements, prepare, 0)
    local_slots(start, 0)
    spread(1)

    def keep(part):
        def done(i, total):
            mid[part, i] = total
        return done

    def finish(part):
        def done(i, total):
            out[i, :, part * lanes:(part + 1) * lanes] = 2.0 * total - start[part, i]
        return done

    halo_slots(0, 0, keep(0))
    for s in range(n):
        for copy in halo(1, 0, s):
            copy.start()
    local_slots(start, 1)
    halo_slots(0, 1, keep(1))
    for s in range(n):
        for copy in halo(1, 1, s):
            copy.start()
    local_slots(mid, 0)
    halo_slots(1, 0, finish(0))
    local_slots(mid, 1)
    halo_slots(1, 1, finish(1))

    for part in range(PARTS):
        for s in range(n):
            for stage in range(2):
                for copy in halo(stage, part, s):
                    copy.wait_send()

            @pl.when((s <= z) & (z < n - 1))
            def _():
                up(part, s).wait_send()

            @pl.when((s >= z) & (z > 0))
            def _():
                down(part, s).wait_send()

        for s in others:
            over_y(part, s).wait_send()
            for far in range(2):
                over_core(part, s, far).wait_send()
            to_band(part, s).wait_send()


def shards(orbitals, rotation, counts, hamiltonian, filter_center, filter_width):
    elements, rows, bands = orbitals.shape
    basis = hamiltonian.shape[2]
    depth = rotation.shape[0]
    n = bands // depth
    lanes = depth // PARTS
    own = (PARTS, elements, basis, lanes)
    dma = pltpu.SemaphoreType.DMA
    in_vmem = pl.BlockSpec(memory_space=pltpu.VMEM)
    in_smem = pl.BlockSpec(memory_space=pltpu.SMEM)
    flops = 2 * elements * rows * bands * bands * 3 + 2 * 2 * elements * SLOTS * basis * basis * depth * 4
    return pl.pallas_call(
        functools.partial(kernel, n),
        out_shape=jax.ShapeDtypeStruct((elements, basis, depth), F32),
        in_specs=[in_vmem, in_vmem, in_smem, in_smem, in_smem, pl.BlockSpec(memory_space=pl.ANY)],
        out_specs=in_vmem,
        scratch_shapes=[
            pltpu.VMEM((elements, SLOTS, basis, basis), F32),
            pltpu.VMEM((elements, SLOTS, 2 * basis, basis), BF16),
            pltpu.VMEM((2 * elements * rows, bands), BF16),
            pltpu.VMEM((PARTS, n, depth, n * lanes), F32),
            pltpu.VMEM((PARTS, n, elements, rows, lanes), F32),
            pltpu.VMEM((PARTS, elements * rows, n * lanes), F32),
            pltpu.VMEM(own, F32), pltpu.VMEM(own, F32), pltpu.VMEM(own, F32),
            pltpu.VMEM(own, F32), pltpu.VMEM(own, F32), pltpu.VMEM(own, F32),
            pltpu.VMEM((3, elements, basis, 2 * lanes), BF16),
            pltpu.VMEM(own, F32),
            dma(()),
            dma((PARTS, n)), dma((PARTS, n)), dma((PARTS, n)),
            dma((PARTS, n)), dma((PARTS, n)),
            dma((PARTS, n, 2)), dma((PARTS, n, 2)),
            dma((PARTS, n)), dma((PARTS, n)),
            dma((2, PARTS, n, 2)), dma((2, PARTS, n, 2)),
        ],
        compiler_params=pltpu.CompilerParams(
            collective_id=0, has_side_effects=True, vmem_limit_bytes=48 * 1024 * 1024
        ),
        cost_estimate=pl.CostEstimate(flops=flops, bytes_accessed=8 * 1024 * 1024, transcendentals=0),
    )(orbitals.reshape(elements * rows, bands), rotation, counts, filter_center, filter_width, hamiltonian)


def solution(mesh):
    fits = mesh.shape["elem"] == GY and mesh.shape["band"] == 4
    return jax.shard_map(
        shards if fits else general_shards,
        mesh=mesh,
        in_specs=(
            P("elem", "band", None),
            P("band", None),
            P("elem"),
            P("elem", None, None, None),
            P(),
            P(),
        ),
        out_specs=P("elem", None, "band"),
        check_vma=False,
    )
```

```python
import functools

import jax
import jax.numpy as jnp
from jax import lax
from jax.experimental import pallas as pl
from jax.experimental.pallas import tpu as pltpu
from jax.sharding import PartitionSpec as P

GY = 8


def neighbour_rows(field, stride, span, wraps):
    size = lax.axis_size("elem")
    behind, ahead = [], []
    for i in range(size):
        place = (i // stride) % span
        base = i - place * stride
        if wraps or place + 1 < span:
            behind.append((i, base + (place + 1) % span * stride))
        if wraps or place > 0:
            ahead.append((i, base + (place + span - 1) % span * stride))
    return lax.ppermute(field, "elem", behind), lax.ppermute(field, "elem", ahead)


def apply_operator(field, hamiltonian, live):
    layers = lax.axis_size("elem") // GY
    others = [field, jnp.roll(field, 1, axis=0), jnp.roll(field, -1, axis=0)]
    others += neighbour_rows(field, 1, GY, True)
    if layers > 1:
        others += neighbour_rows(field, GY, layers, False)
    total = jnp.zeros(field.shape, jnp.float32)
    for slot, other in enumerate(others):
        total = total + jnp.einsum(
            "erc,ecb->erb", hamiltonian[:, slot], other, precision=lax.Precision.HIGH
        )
    return jnp.where(live[:, :, None], total, jnp.float32(0.0))


def general_shards(orbitals, rotation, counts, hamiltonian, filter_center, filter_width):
    elements, rows_here, bands = orbitals.shape
    basis = hamiltonian.shape[2]
    whole_rotation = lax.all_gather(rotation, "band", axis=0, tiled=True)
    rotated = jnp.einsum(
        "eik,kb->eib", orbitals, whole_rotation, precision=lax.Precision.HIGH
    )
    start = lax.all_to_all(rotated, "band", split_axis=2, concat_axis=1, tiled=True)
    live = jnp.arange(basis, dtype=jnp.int32)[None, :] < counts[:, None]
    start = jnp.where(live[:, :, None], start, jnp.float32(0.0))
    center = filter_center[0]
    width = filter_width[0]
    middle = (apply_operator(start, hamiltonian, live) - center * start) / width
    return 2.0 * (apply_operator(middle, hamiltonian, live) - center * middle) / width - start


F32, BF16 = jnp.float32, jnp.bfloat16
PARTS = 2
SLOTS = 5


def split(x):
    high = x.astype(BF16)
    return high, (x - high.astype(F32)).astype(BF16)


def kernel(
    n, orb, rot, counts, center, width, ham, out,
    ham_v, ham_b, orb_v, orb_b, rot_b, res, acc_r, start, start_lo, start_hi, mid, mid_lo, mid_hi,
    field, acc, ham_sem, orb_sem, rot_sem,
    up_s, dn_s, z_r, y_s, y_r, c_s, c_r, a_s, a_r, h_s, h_r,
):
    e, z = lax.axis_index("elem"), lax.axis_index("band")
    elements, basis = ham.shape[0], ham.shape[2]
    rows = basis // n
    depth = rot.shape[0]
    lanes = start.shape[3]
    share = depth // 4
    y, c = e // 4, e % 2
    ahead, behind = lax.rem(e + 1, 8), lax.rem(e + 7, 8)
    across, twin = lax.rem(e + 4, 8), e + 1 - 2 * c
    others = [lax.rem(z + j, n) for j in range(1, n)]

    def remote(src, dst, send, recv, elem, band):
        return pltpu.make_async_remote_copy(
            src_ref=src, dst_ref=dst, send_sem=send, recv_sem=recv,
            device_id=(elem, band), device_id_type=pl.DeviceIdType.MESH,
        )

    def block(ref, part, s, yy, cc):
        first = pl.multiple_of((yy * 2 + cc) * share, share)
        return ref.at[part, s, pl.ds(first, share)]

    def up(part, s):
        b = block(rot_b, part, s, y, c)
        return remote(b, b, up_s.at[part, s], z_r.at[part, s], e, z + 1)

    def down(part, s):
        b = block(rot_b, part, s, y, c)
        return remote(b, b, dn_s.at[part, s], z_r.at[part, s], e, z - 1)

    def over_y(part, s):
        b = block(rot_b, part, s, y, c)
        return remote(b, b, y_s.at[part, s], y_r.at[part, s], across, z)

    def over_core(part, s, far):
        yy = 1 - y if far else y
        b = block(rot_b, part, s, yy, c)
        return remote(b, b, c_s.at[part, s, far], c_r.at[part, s, far], twin, z)

    def got(dst, recv):
        remote(dst, dst, recv, recv, twin, z).wait_recv()

    def rows_of(part, i, s):
        return start.at[part, i, pl.ds(pl.multiple_of(s * rows, rows), rows)]

    def to_band(part, i, to):
        return remote(
            res.at[part, to, i], rows_of(part, i, z), a_s.at[part, i, to], a_r.at[part, i, z], e, to
        )

    def halo(stage, part, i):
        own, lo, hi = ((start, start_lo, start_hi), (mid, mid_lo, mid_hi))[stage]
        b = own.at[part, i]
        return (
            remote(b, lo.at[part, i], h_s.at[stage, part, i, 0], h_r.at[stage, part, i, 0], ahead, z),
            remote(b, hi.at[part, i], h_s.at[stage, part, i, 1], h_r.at[stage, part, i, 1], behind, z),
        )

    barrier = pltpu.get_barrier_semaphore()
    partners = [(ahead, z), (behind, z), (across, z)] + [(e, other) for other in others]
    for elem, band in partners:
        pl.semaphore_signal(barrier, inc=1, device_id=(elem, band), device_id_type=pl.DeviceIdType.MESH)
    ham_copy = pltpu.make_async_copy(ham.at[:, pl.ds(0, SLOTS)], ham_v, ham_sem)
    orb_copy = pltpu.make_async_copy(orb, orb_v, orb_sem)
    rot_copies = [
        pltpu.make_async_copy(
            rot.at[:, pl.ds((b * PARTS + part) * lanes, lanes)],
            rot_b.at[part, z, :, pl.ds(b * lanes, lanes)],
            rot_sem.at[part, b],
        )
        for part in range(PARTS)
        for b in range(n)
    ]
    for copy in rot_copies[:n] + [orb_copy] + rot_copies[n:] + [ham_copy]:
        copy.start()
    pl.semaphore_wait(barrier, len(partners))

    def send_own(part):
        for copy in rot_copies[part * n:(part + 1) * n]:
            copy.wait()

        @pl.when(z < n - 1)
        def _():
            up(part, z).start()

        @pl.when(z > 0)
        def _():
            down(part, z).start()

    def relay(part, d):
        @pl.when(z >= d)
        def _():
            s = z - d
            got(block(rot_b, part, s, y, c), z_r.at[part, s])

            @pl.when(z < n - 1)
            def _():
                up(part, s).start()

            over_y(part, s).start()
            over_core(part, s, 0).start()

        @pl.when(z + d < n)
        def _():
            s = z + d
            got(block(rot_b, part, s, y, c), z_r.at[part, s])

            @pl.when(z > 0)
            def _():
                down(part, s).start()

            over_y(part, s).start()
            over_core(part, s, 0).start()

    def relay_y(part):
        for s in others:
            got(block(rot_b, part, s, 1 - y, c), y_r.at[part, s])
            over_core(part, s, 1).start()

    def rotate(part, s, first):
        columns = pl.ds(pl.multiple_of(s * depth, depth), depth)
        high, low = split(rot_b[part, s])
        both = jnp.dot(orb_b[:, columns], high, preferred_element_type=F32)
        cross = jnp.dot(orb_b[:elements * rows, columns], low, preferred_element_type=F32)
        total = both[:elements * rows] + both[elements * rows:] + cross
        acc_r[part] = total if first else acc_r[part] + total

    def rotated(part):
        for s in others:
            for far in range(2):
                got(block(rot_b, part, s, 1 - y if far else y, 1 - c), c_r.at[part, s, far])
            rotate(part, s, False)
        for i in range(elements):
            place = lax.broadcasted_iota(jnp.int32, (rows, lanes), 0) + z * rows
            alive = place < counts[i]
            for b in range(n):
                piece = acc_r[part, i * rows:(i + 1) * rows, b * lanes:(b + 1) * lanes]
                res[part, b, i] = jnp.where(alive, piece, F32(0.0))
            for to in others:
                to_band(part, i, to).start()
            start[part, i, pl.ds(pl.multiple_of(z * rows, rows), rows)] = res[part, z, i]

    def spread(part, i):
        for s in others:
            got(rows_of(part, i, s), a_r.at[part, i, s])
        for copy in halo(0, part, i):
            copy.start()

    def load(k, ref, part, i):
        high, low = split(ref[part, i])
        field[k, i, :, :lanes] = high
        field[k, i, :, lanes:] = low

    def fold(r):
        return (r[:basis, :lanes] + r[:basis, lanes:]) + (r[basis:, :lanes] + r[basis:, lanes:])

    def local_slots(ref, part):
        for i in range(elements):
            load(0, ref, part, i)

        def body(i, carry):
            r = jnp.dot(ham_b[i, 0], field[0, i], preferred_element_type=F32)
            r += jnp.dot(ham_b[i, 1], field[0, lax.rem(i + elements - 1, elements)], preferred_element_type=F32)
            r += jnp.dot(ham_b[i, 2], field[0, lax.rem(i + 1, elements)], preferred_element_type=F32)
            acc[part, i] = fold(r)
            return carry

        lax.fori_loop(0, elements, body, 0)

    def halo_slots(stage, part, i):
        lo, hi = ((start_lo, start_hi), (mid_lo, mid_hi))[stage]
        got(lo.at[part, i], h_r.at[stage, part, i, 0])
        got(hi.at[part, i], h_r.at[stage, part, i, 1])
        load(1, lo, part, i)
        load(2, hi, part, i)
        r = jnp.dot(ham_b[i, 3], field[1, i], preferred_element_type=F32)
        r += jnp.dot(ham_b[i, 4], field[2, i], preferred_element_type=F32)
        return acc[part, i] + fold(r)

    def middle(part, i):
        mid[part, i] = halo_slots(0, part, i)
        for copy in halo(1, part, i):
            copy.start()

    def finish(part, i):
        out[i, :, part * lanes:(part + 1) * lanes] = 2.0 * halo_slots(1, part, i) - start[part, i]

    def prepare_all():
        ham_copy.wait()

        def prepare(i, carry):
            square = (basis, basis)
            place = lax.broadcasted_iota(jnp.int32, square, 0)
            scale = jnp.where(place < counts[i], 1.0 / jnp.full(square, width[0], F32), F32(0.0))
            diagonal = jnp.where(place == lax.broadcasted_iota(jnp.int32, square, 1), center[0], F32(0.0))
            for slot in range(SLOTS):
                entries = ham_v[i, slot]
                if slot == 0:
                    entries = entries - diagonal
                high, low = split(entries * scale)
                ham_b[i, slot, :basis] = high
                ham_b[i, slot, basis:] = low
            return carry

        lax.fori_loop(0, elements, prepare, 0)

    send_own(0)
    orb_copy.wait()
    high, low = split(orb_v[...])
    orb_b[:elements * rows] = high
    orb_b[elements * rows:] = low
    rotate(0, z, True)
    relay(0, 1)
    relay(0, 2)
    send_own(1)
    relay(0, 3)
    prepare_all()
    relay_y(0)
    rotated(0)
    relay(1, 1)
    relay(1, 2)
    relay(1, 3)
    rotate(1, z, True)
    relay_y(1)
    spread(0, 0)
    spread(0, 1)
    rotated(1)
    for i in range(2, elements):
        spread(0, i)
    local_slots(start, 0)
    for i in range(elements):
        middle(0, i)
        spread(1, i)
    local_slots(start, 1)
    for i in range(elements):
        middle(1, i)
    local_slots(mid, 0)
    for i in range(elements):
        finish(0, i)
    local_slots(mid, 1)
    for i in range(elements):
        finish(1, i)

    for part in range(PARTS):
        for i in range(elements):
            for stage in range(2):
                for copy in halo(stage, part, i):
                    copy.wait_send()
            for to in others:
                to_band(part, i, to).wait_send()
        for s in range(n):
            @pl.when((s <= z) & (z < n - 1))
            def _():
                up(part, s).wait_send()

            @pl.when((s >= z) & (z > 0))
            def _():
                down(part, s).wait_send()

        for s in others:
            over_y(part, s).wait_send()
            for far in range(2):
                over_core(part, s, far).wait_send()


def shards(orbitals, rotation, counts, hamiltonian, filter_center, filter_width):
    elements, rows, bands = orbitals.shape
    basis = hamiltonian.shape[2]
    depth = rotation.shape[0]
    n = bands // depth
    lanes = depth // PARTS
    own = (PARTS, elements, basis, lanes)
    dma = pltpu.SemaphoreType.DMA
    in_vmem = pl.BlockSpec(memory_space=pltpu.VMEM)
    in_hbm = pl.BlockSpec(memory_space=pltpu.HBM)
    in_smem = pl.BlockSpec(memory_space=pltpu.SMEM)
    flops = 2 * elements * rows * bands * bands * 3 + 2 * 2 * elements * SLOTS * basis * basis * depth * 4
    return pl.pallas_call(
        functools.partial(kernel, n),
        out_shape=jax.ShapeDtypeStruct((elements, basis, depth), F32),
        in_specs=[in_hbm, in_hbm, in_smem, in_smem, in_smem, in_hbm],
        out_specs=in_vmem,
        scratch_shapes=[
            pltpu.VMEM((elements, SLOTS, basis, basis), F32),
            pltpu.VMEM((elements, SLOTS, 2 * basis, basis), BF16),
            pltpu.VMEM((elements * rows, bands), F32),
            pltpu.VMEM((2 * elements * rows, bands), BF16),
            pltpu.VMEM((PARTS, n, depth, n * lanes), F32),
            pltpu.VMEM((PARTS, n, elements, rows, lanes), F32),
            pltpu.VMEM((PARTS, elements * rows, n * lanes), F32),
            pltpu.VMEM(own, F32), pltpu.VMEM(own, F32), pltpu.VMEM(own, F32),
            pltpu.VMEM(own, F32), pltpu.VMEM(own, F32), pltpu.VMEM(own, F32),
            pltpu.VMEM((3, elements, basis, 2 * lanes), BF16),
            pltpu.VMEM(own, F32),
            dma(()), dma(()), dma((PARTS, n)),
            dma((PARTS, n)), dma((PARTS, n)), dma((PARTS, n)),
            dma((PARTS, n)), dma((PARTS, n)),
            dma((PARTS, n, 2)), dma((PARTS, n, 2)),
            dma((PARTS, elements, n)), dma((PARTS, elements, n)),
            dma((2, PARTS, elements, 2)), dma((2, PARTS, elements, 2)),
        ],
        compiler_params=pltpu.CompilerParams(
            collective_id=0, has_side_effects=True, vmem_limit_bytes=63 * 1024 * 1024
        ),
        cost_estimate=pl.CostEstimate(flops=flops, bytes_accessed=8 * 1024 * 1024, transcendentals=0),
    )(orbitals.reshape(elements * rows, bands), rotation, counts, filter_center, filter_width, hamiltonian)


def solution(mesh):
    fits = mesh.shape["elem"] == GY and mesh.shape["band"] == 4
    return jax.shard_map(
        shards if fits else general_shards,
        mesh=mesh,
        in_specs=(
            P("elem", "band", None),
            P("band", None),
            P("elem"),
            P("elem", None, None, None),
            P(),
            P(),
        ),
        out_specs=P("elem", None, "band"),
        check_vma=False,
    )
```

```python
import functools

import jax
import jax.numpy as jnp
from jax import lax
from jax.experimental import pallas as pl
from jax.experimental.pallas import tpu as pltpu
from jax.sharding import PartitionSpec as P

GY = 8


def neighbour_rows(field, stride, span, wraps):
    size = lax.axis_size("elem")
    behind, ahead = [], []
    for i in range(size):
        place = (i // stride) % span
        base = i - place * stride
        if wraps or place + 1 < span:
            behind.append((i, base + (place + 1) % span * stride))
        if wraps or place > 0:
            ahead.append((i, base + (place + span - 1) % span * stride))
    return lax.ppermute(field, "elem", behind), lax.ppermute(field, "elem", ahead)


def apply_operator(field, hamiltonian, live):
    layers = lax.axis_size("elem") // GY
    others = [field, jnp.roll(field, 1, axis=0), jnp.roll(field, -1, axis=0)]
    others += neighbour_rows(field, 1, GY, True)
    if layers > 1:
        others += neighbour_rows(field, GY, layers, False)
    total = jnp.zeros(field.shape, jnp.float32)
    for slot, other in enumerate(others):
        total = total + jnp.einsum(
            "erc,ecb->erb", hamiltonian[:, slot], other, precision=lax.Precision.HIGH
        )
    return jnp.where(live[:, :, None], total, jnp.float32(0.0))


def general_shards(orbitals, rotation, counts, hamiltonian, filter_center, filter_width):
    elements, rows_here, bands = orbitals.shape
    basis = hamiltonian.shape[2]
    whole_rotation = lax.all_gather(rotation, "band", axis=0, tiled=True)
    rotated = jnp.einsum(
        "eik,kb->eib", orbitals, whole_rotation, precision=lax.Precision.HIGH
    )
    start = lax.all_to_all(rotated, "band", split_axis=2, concat_axis=1, tiled=True)
    live = jnp.arange(basis, dtype=jnp.int32)[None, :] < counts[:, None]
    start = jnp.where(live[:, :, None], start, jnp.float32(0.0))
    center = filter_center[0]
    width = filter_width[0]
    middle = (apply_operator(start, hamiltonian, live) - center * start) / width
    return 2.0 * (apply_operator(middle, hamiltonian, live) - center * middle) / width - start


F32, BF16 = jnp.float32, jnp.bfloat16
PARTS = 2
SLOTS = 5


def split(x):
    high = x.astype(BF16)
    return high, (x - high.astype(F32)).astype(BF16)


def kernel(
    n, orb, rot, counts, center, width, ham, out,
    ham_v, ham_b, orb_v, orb_b, rot_b, res, acc_r, start, start_lo, start_hi, mid, mid_lo, mid_hi,
    field, acc, ham_sem, orb_sem, rot_sem,
    g_s, g_r, c_s, c_r, a_s, a_r, b_s, b_r, h_s, h_r,
):
    e, z = lax.axis_index("elem"), lax.axis_index("band")
    elements, basis = ham.shape[0], ham.shape[2]
    rows = basis // n
    depth = rot.shape[0]
    lanes = start.shape[3]
    share = depth // 8
    x, c = (e // 2) % 2, e % 2
    ahead, behind = lax.rem(e + 1, 8), lax.rem(e + 7, 8)
    beside, across, twin = e + 2 - 4 * x, lax.rem(e + 4, 8), e + 1 - 2 * c
    diagonal = lax.rem(beside + 4, 8)
    planes = (e, beside, across, diagonal)
    others = [lax.rem(z + j, n) for j in range(1, n)]

    def remote(src, dst, send, recv, elem, band):
        return pltpu.make_async_remote_copy(
            src_ref=src, dst_ref=dst, send_sem=send, recv_sem=recv,
            device_id=(elem, band), device_id_type=pl.DeviceIdType.MESH,
        )

    def eighth(part, s, owner):
        return rot_b.at[part, s, pl.ds(pl.multiple_of(owner * share, share), share)]

    def over_z(part, to):
        b = eighth(part, z, e)
        return remote(b, b, g_s.at[0, part, to], g_r.at[0, part, z], e, to)

    def over_x(part, s):
        b = eighth(part, s, e)
        return remote(b, b, g_s.at[1, part, s], g_r.at[1, part, s], beside, z)

    def over_y(part, s):
        b = eighth(part, s, e)
        return remote(b, b, g_s.at[2, part, s], g_r.at[2, part, s], across, z)

    def relay_over_y(part, s):
        b = eighth(part, s, beside)
        return remote(b, b, g_s.at[3, part, s], g_r.at[3, part, s], across, z)

    def relay_over_x(part, s):
        b = eighth(part, s, across)
        return remote(b, b, g_s.at[3, part, s], g_r.at[3, part, s], beside, z)

    def over_core(part, s, k):
        b = eighth(part, s, planes[k])
        return remote(b, b, c_s.at[part, s, k], c_r.at[part, s, k], twin, z)

    def got(dst, recv):
        remote(dst, dst, recv, recv, twin, z).wait_recv()

    def rows_of(ref, part, s):
        return ref.at[part, :, pl.ds(pl.multiple_of(s * rows, rows), rows)]

    def to_band(part, to):
        return remote(res.at[part, to], rows_of(start, part, z), a_s.at[part, to], a_r.at[part, z], e, to)

    def start_halo(part, s):
        b = rows_of(start, part, s)
        return (
            remote(b, rows_of(start_lo, part, s), b_s.at[part, s, 0], b_r.at[part, s, 0], ahead, z),
            remote(b, rows_of(start_hi, part, s), b_s.at[part, s, 1], b_r.at[part, s, 1], behind, z),
        )

    def mid_halo(part, i):
        b = mid.at[part, i]
        return (
            remote(b, mid_lo.at[part, i], h_s.at[part, i, 0], h_r.at[part, i, 0], ahead, z),
            remote(b, mid_hi.at[part, i], h_s.at[part, i, 1], h_r.at[part, i, 1], behind, z),
        )

    barrier = pltpu.get_barrier_semaphore()
    partners = [(ahead, z), (behind, z), (beside, z), (across, z)] + [(e, other) for other in others]
    for elem, band in partners:
        pl.semaphore_signal(barrier, inc=1, device_id=(elem, band), device_id_type=pl.DeviceIdType.MESH)
    ham_copy = pltpu.make_async_copy(ham.at[:, pl.ds(0, SLOTS)], ham_v, ham_sem)
    orb_copy = pltpu.make_async_copy(orb, orb_v, orb_sem)
    rot_copies = [
        pltpu.make_async_copy(
            rot.at[:, pl.ds((b * PARTS + part) * lanes, lanes)],
            rot_b.at[part, z, :, pl.ds(b * lanes, lanes)],
            rot_sem.at[part, b],
        )
        for part in range(PARTS)
        for b in range(n)
    ]
    for copy in rot_copies[:n] + [orb_copy] + rot_copies[n:] + [ham_copy]:
        copy.start()
    pl.semaphore_wait(barrier, len(partners))

    def send_own(part):
        for copy in rot_copies[part * n:(part + 1) * n]:
            copy.wait()
        for to in others:
            over_z(part, to).start()

    def gather_first(part):
        for s in others:
            got(eighth(part, s, e), g_r.at[0, part, s])
            over_x(part, s).start()
            over_y(part, s).start()
            over_core(part, s, 0).start()

    def gather_second(part):
        for s in others:
            got(eighth(part, s, beside), g_r.at[1, part, s])
            got(eighth(part, s, across), g_r.at[2, part, s])

            @pl.when(c == 0)
            def _():
                relay_over_y(part, s).start()

            @pl.when(c == 1)
            def _():
                relay_over_x(part, s).start()

            over_core(part, s, 1).start()
            over_core(part, s, 2).start()

    def gather_third(part):
        for s in others:
            got(eighth(part, s, diagonal), g_r.at[3, part, s])
            over_core(part, s, 3).start()

    def rotate(part, s, first):
        columns = pl.ds(pl.multiple_of(s * depth, depth), depth)
        high, low = split(rot_b[part, s])
        both = jnp.dot(orb_b[:, columns], high, preferred_element_type=F32)
        cross = jnp.dot(orb_b[:elements * rows, columns], low, preferred_element_type=F32)
        total = both[:elements * rows] + both[elements * rows:] + cross
        acc_r[part] = total if first else acc_r[part] + total

    def rotated(part):
        for s in others:
            for k in range(4):
                got(eighth(part, s, planes[k] + 1 - 2 * c), c_r.at[part, s, k])
            rotate(part, s, False)
        for i in range(elements):
            place = lax.broadcasted_iota(jnp.int32, (rows, lanes), 0) + z * rows
            alive = place < counts[i]
            for b in range(n):
                piece = acc_r[part, i * rows:(i + 1) * rows, b * lanes:(b + 1) * lanes]
                res[part, b, i] = jnp.where(alive, piece, F32(0.0))
        for to in others:
            to_band(part, to).start()
        start[part, :, pl.ds(pl.multiple_of(z * rows, rows), rows)] = res[part, z]
        for copy in start_halo(part, z):
            copy.start()

    def spread(part):
        for s in others:
            got(rows_of(start, part, s), a_r.at[part, s])
            for copy in start_halo(part, s):
                copy.start()

    def load(k, ref, part, i):
        high, low = split(ref[part, i])
        field[k, i, :, :lanes] = high
        field[k, i, :, lanes:] = low

    def fold(r):
        return (r[:basis, :lanes] + r[:basis, lanes:]) + (r[basis:, :lanes] + r[basis:, lanes:])

    def local_slots(ref, part):
        for i in range(elements):
            load(0, ref, part, i)

        def body(i, carry):
            r = jnp.dot(ham_b[i, 0], field[0, i], preferred_element_type=F32)
            r += jnp.dot(ham_b[i, 1], field[0, lax.rem(i + elements - 1, elements)], preferred_element_type=F32)
            r += jnp.dot(ham_b[i, 2], field[0, lax.rem(i + 1, elements)], preferred_element_type=F32)
            acc[part, i] = fold(r)
            return carry

        lax.fori_loop(0, elements, body, 0)

    def halo_slots(lo, hi, part, i):
        load(1, lo, part, i)
        load(2, hi, part, i)
        r = jnp.dot(ham_b[i, 3], field[1, i], preferred_element_type=F32)
        r += jnp.dot(ham_b[i, 4], field[2, i], preferred_element_type=F32)
        return acc[part, i] + fold(r)

    def middle(part):
        for s in range(n):
            got(rows_of(start_lo, part, s), b_r.at[part, s, 0])
            got(rows_of(start_hi, part, s), b_r.at[part, s, 1])
        for i in range(elements):
            mid[part, i] = halo_slots(start_lo, start_hi, part, i)
            for copy in mid_halo(part, i):
                copy.start()

    def finish(part):
        for i in range(elements):
            got(mid_lo.at[part, i], h_r.at[part, i, 0])
            got(mid_hi.at[part, i], h_r.at[part, i, 1])
            total = halo_slots(mid_lo, mid_hi, part, i)
            out[i, :, part * lanes:(part + 1) * lanes] = 2.0 * total - start[part, i]

    def prepare_all():
        ham_copy.wait()

        def prepare(i, carry):
            square = (basis, basis)
            place = lax.broadcasted_iota(jnp.int32, square, 0)
            scale = jnp.where(place < counts[i], 1.0 / jnp.full(square, width[0], F32), F32(0.0))
            diagonal = jnp.where(place == lax.broadcasted_iota(jnp.int32, square, 1), center[0], F32(0.0))
            for slot in range(SLOTS):
                entries = ham_v[i, slot]
                if slot == 0:
                    entries = entries - diagonal
                high, low = split(entries * scale)
                ham_b[i, slot, :basis] = high
                ham_b[i, slot, basis:] = low
            return carry

        lax.fori_loop(0, elements, prepare, 0)

    send_own(0)
    send_own(1)
    orb_copy.wait()
    high, low = split(orb_v[...])
    orb_b[:elements * rows] = high
    orb_b[elements * rows:] = low
    rotate(0, z, True)
    gather_first(0)
    gather_second(0)
    gather_first(1)
    gather_third(0)
    gather_second(1)
    rotated(0)
    gather_third(1)
    rotate(1, z, True)
    rotated(1)
    spread(0)
    prepare_all()
    local_slots(start, 0)
    spread(1)
    middle(0)
    local_slots(start, 1)
    middle(1)
    local_slots(mid, 0)
    finish(0)
    local_slots(mid, 1)
    finish(1)

    for part in range(PARTS):
        for i in range(elements):
            for copy in mid_halo(part, i):
                copy.wait_send()
        for s in range(n):
            for copy in start_halo(part, s):
                copy.wait_send()
        for s in others:
            over_z(part, s).wait_send()
            over_x(part, s).wait_send()
            over_y(part, s).wait_send()
            relay_over_y(part, s).wait_send()
            for k in range(4):
                over_core(part, s, k).wait_send()
            to_band(part, s).wait_send()


def shards(orbitals, rotation, counts, hamiltonian, filter_center, filter_width):
    elements, rows, bands = orbitals.shape
    basis = hamiltonian.shape[2]
    depth = rotation.shape[0]
    n = bands // depth
    lanes = depth // PARTS
    own = (PARTS, elements, basis, lanes)
    dma = pltpu.SemaphoreType.DMA
    in_vmem = pl.BlockSpec(memory_space=pltpu.VMEM)
    in_hbm = pl.BlockSpec(memory_space=pltpu.HBM)
    in_smem = pl.BlockSpec(memory_space=pltpu.SMEM)
    flops = 2 * elements * rows * bands * bands * 3 + 2 * 2 * elements * SLOTS * basis * basis * depth * 4
    return pl.pallas_call(
        functools.partial(kernel, n),
        out_shape=jax.ShapeDtypeStruct((elements, basis, depth), F32),
        in_specs=[in_hbm, in_hbm, in_smem, in_smem, in_smem, in_hbm],
        out_specs=in_vmem,
        scratch_shapes=[
            pltpu.VMEM((elements, SLOTS, basis, basis), F32),
            pltpu.VMEM((elements, SLOTS, 2 * basis, basis), BF16),
            pltpu.VMEM((elements * rows, bands), F32),
            pltpu.VMEM((2 * elements * rows, bands), BF16),
            pltpu.VMEM((PARTS, n, depth, n * lanes), F32),
            pltpu.VMEM((PARTS, n, elements, rows, lanes), F32),
            pltpu.VMEM((PARTS, elements * rows, n * lanes), F32),
            pltpu.VMEM(own, F32), pltpu.VMEM(own, F32), pltpu.VMEM(own, F32),
            pltpu.VMEM(own, F32), pltpu.VMEM(own, F32), pltpu.VMEM(own, F32),
            pltpu.VMEM((3, elements, basis, 2 * lanes), BF16),
            pltpu.VMEM(own, F32),
            dma(()), dma(()), dma((PARTS, n)),
            dma((4, PARTS, n)), dma((4, PARTS, n)),
            dma((PARTS, n, 4)), dma((PARTS, n, 4)),
            dma((PARTS, n)), dma((PARTS, n)),
            dma((PARTS, n, 2)), dma((PARTS, n, 2)),
            dma((PARTS, elements, 2)), dma((PARTS, elements, 2)),
        ],
        compiler_params=pltpu.CompilerParams(
            collective_id=0, has_side_effects=True, vmem_limit_bytes=63 * 1024 * 1024
        ),
        cost_estimate=pl.CostEstimate(flops=flops, bytes_accessed=8 * 1024 * 1024, transcendentals=0),
    )(orbitals.reshape(elements * rows, bands), rotation, counts, filter_center, filter_width, hamiltonian)


def solution(mesh):
    fits = mesh.shape["elem"] == GY and mesh.shape["band"] == 4
    return jax.shard_map(
        shards if fits else general_shards,
        mesh=mesh,
        in_specs=(
            P("elem", "band", None),
            P("band", None),
            P("elem"),
            P("elem", None, None, None),
            P(),
            P(),
        ),
        out_specs=P("elem", None, "band"),
        check_vma=False,
    )
```

```python
import functools

import jax
import jax.numpy as jnp
from jax import lax
from jax.experimental import pallas as pl
from jax.experimental.pallas import tpu as pltpu
from jax.sharding import PartitionSpec as P

GY = 8


def neighbour_rows(field, stride, span, wraps):
    size = lax.axis_size("elem")
    behind, ahead = [], []
    for i in range(size):
        place = (i // stride) % span
        base = i - place * stride
        if wraps or place + 1 < span:
            behind.append((i, base + (place + 1) % span * stride))
        if wraps or place > 0:
            ahead.append((i, base + (place + span - 1) % span * stride))
    return lax.ppermute(field, "elem", behind), lax.ppermute(field, "elem", ahead)


def apply_operator(field, hamiltonian, live):
    layers = lax.axis_size("elem") // GY
    others = [field, jnp.roll(field, 1, axis=0), jnp.roll(field, -1, axis=0)]
    others += neighbour_rows(field, 1, GY, True)
    if layers > 1:
        others += neighbour_rows(field, GY, layers, False)
    total = jnp.zeros(field.shape, jnp.float32)
    for slot, other in enumerate(others):
        total = total + jnp.einsum(
            "erc,ecb->erb", hamiltonian[:, slot], other, precision=lax.Precision.HIGH
        )
    return jnp.where(live[:, :, None], total, jnp.float32(0.0))


def general_shards(orbitals, rotation, counts, hamiltonian, filter_center, filter_width):
    elements, rows_here, bands = orbitals.shape
    basis = hamiltonian.shape[2]
    whole_rotation = lax.all_gather(rotation, "band", axis=0, tiled=True)
    rotated = jnp.einsum(
        "eik,kb->eib", orbitals, whole_rotation, precision=lax.Precision.HIGH
    )
    start = lax.all_to_all(rotated, "band", split_axis=2, concat_axis=1, tiled=True)
    live = jnp.arange(basis, dtype=jnp.int32)[None, :] < counts[:, None]
    start = jnp.where(live[:, :, None], start, jnp.float32(0.0))
    center = filter_center[0]
    width = filter_width[0]
    middle = (apply_operator(start, hamiltonian, live) - center * start) / width
    return 2.0 * (apply_operator(middle, hamiltonian, live) - center * middle) / width - start


F32, BF16 = jnp.float32, jnp.bfloat16
PARTS = 2
SLOTS = 5


def split(x):
    high = x.astype(BF16)
    return high, (x - high.astype(F32)).astype(BF16)


def kernel(
    n, orb, rot, counts, center, width, ham, out,
    ham_v, ham_b, orb_v, orb_b, rot_b, res, acc_r, start, start_lo, start_hi, mid, mid_lo, mid_hi,
    field, acc, ham_sem, orb_sem, rot_sem,
    g_s, g_r, c_s, c_r, a_s, a_r, b_s, b_r, h_s, h_r,
):
    e, z = lax.axis_index("elem"), lax.axis_index("band")
    elements, basis = ham.shape[0], ham.shape[2]
    rows = basis // n
    depth = rot.shape[0]
    lanes = start.shape[3]
    share = depth // 8
    x, c = (e // 2) % 2, e % 2
    ahead, behind = lax.rem(e + 1, 8), lax.rem(e + 7, 8)
    beside, across, twin = e + 2 - 4 * x, lax.rem(e + 4, 8), e + 1 - 2 * c
    diagonal = lax.rem(beside + 4, 8)
    planes = (e, beside, across, diagonal)
    others = [z + 1 - 2 * (z // 2), lax.rem(2 + 3 * z, 5), 3 - 3 * (z // 2)]

    def remote(src, dst, send, recv, elem, band):
        return pltpu.make_async_remote_copy(
            src_ref=src, dst_ref=dst, send_sem=send, recv_sem=recv,
            device_id=(elem, band), device_id_type=pl.DeviceIdType.MESH,
        )

    def eighth(part, s, owner):
        return rot_b.at[part, s, pl.ds(pl.multiple_of(owner * share, share), share)]

    def over_z(part, to):
        b = eighth(part, z, e)
        return remote(b, b, g_s.at[0, part, to], g_r.at[0, part, z], e, to)

    def over_x(part, s):
        b = eighth(part, s, e)
        return remote(b, b, g_s.at[1, part, s], g_r.at[1, part, s], beside, z)

    def over_y(part, s):
        b = eighth(part, s, e)
        return remote(b, b, g_s.at[2, part, s], g_r.at[2, part, s], across, z)

    def relay_over_y(part, s):
        b = eighth(part, s, beside)
        return remote(b, b, g_s.at[3, part, s], g_r.at[3, part, s], across, z)

    def relay_over_x(part, s):
        b = eighth(part, s, across)
        return remote(b, b, g_s.at[3, part, s], g_r.at[3, part, s], beside, z)

    def over_core(part, s, k):
        b = eighth(part, s, planes[k])
        return remote(b, b, c_s.at[part, s, k], c_r.at[part, s, k], twin, z)

    def got(dst, recv):
        remote(dst, dst, recv, recv, twin, z).wait_recv()

    def rows_of(ref, part, s):
        return ref.at[part, :, pl.ds(pl.multiple_of(s * rows, rows), rows)]

    def to_band(part, to):
        return remote(res.at[part, to], rows_of(start, part, z), a_s.at[part, to], a_r.at[part, z], e, to)

    def start_halo(part, s):
        b = rows_of(start, part, s)
        return (
            remote(b, rows_of(start_lo, part, s), b_s.at[part, s, 0], b_r.at[part, s, 0], ahead, z),
            remote(b, rows_of(start_hi, part, s), b_s.at[part, s, 1], b_r.at[part, s, 1], behind, z),
        )

    def mid_halo(part, i):
        b = mid.at[part, i]
        return (
            remote(b, mid_lo.at[part, i], h_s.at[part, i, 0], h_r.at[part, i, 0], ahead, z),
            remote(b, mid_hi.at[part, i], h_s.at[part, i, 1], h_r.at[part, i, 1], behind, z),
        )

    barrier = pltpu.get_barrier_semaphore()
    partners = [(ahead, z), (behind, z), (beside, z), (across, z)] + [(e, other) for other in others]
    for elem, band in partners:
        pl.semaphore_signal(barrier, inc=1, device_id=(elem, band), device_id_type=pl.DeviceIdType.MESH)
    ham_copy = pltpu.make_async_copy(ham.at[:, pl.ds(0, SLOTS)], ham_v, ham_sem)
    orb_copy = pltpu.make_async_copy(orb, orb_v, orb_sem)
    rot_copies = [
        pltpu.make_async_copy(
            rot.at[:, pl.ds((b * PARTS + part) * lanes, lanes)],
            rot_b.at[part, z, :, pl.ds(b * lanes, lanes)],
            rot_sem.at[part, b],
        )
        for part in range(PARTS)
        for b in range(n)
    ]
    for copy in rot_copies[:n] + [orb_copy] + rot_copies[n:] + [ham_copy]:
        copy.start()
    pl.semaphore_wait(barrier, len(partners))

    def send_own(part):
        for copy in rot_copies[part * n:(part + 1) * n]:
            copy.wait()
        for to in others:
            over_z(part, to).start()

    def gather_first(part):
        for s in others:
            got(eighth(part, s, e), g_r.at[0, part, s])
            over_x(part, s).start()
            over_y(part, s).start()
            over_core(part, s, 0).start()

    def gather_second(part):
        for s in others:
            got(eighth(part, s, beside), g_r.at[1, part, s])
            got(eighth(part, s, across), g_r.at[2, part, s])

            @pl.when(c == 0)
            def _():
                relay_over_y(part, s).start()

            @pl.when(c == 1)
            def _():
                relay_over_x(part, s).start()

            over_core(part, s, 1).start()
            over_core(part, s, 2).start()

    def gather_third(part):
        for s in others:
            got(eighth(part, s, diagonal), g_r.at[3, part, s])
            over_core(part, s, 3).start()

    def rotate(part, s, first):
        columns = pl.ds(pl.multiple_of(s * depth, depth), depth)
        high, low = split(rot_b[part, s])
        both = jnp.dot(orb_b[:, columns], high, preferred_element_type=F32)
        cross = jnp.dot(orb_b[:elements * rows, columns], low, preferred_element_type=F32)
        total = both[:elements * rows] + both[elements * rows:] + cross
        acc_r[part] = total if first else acc_r[part] + total

    def rotated(part):
        for s in others:
            for k in range(4):
                got(eighth(part, s, planes[k] + 1 - 2 * c), c_r.at[part, s, k])
            rotate(part, s, False)
        for i in range(elements):
            place = lax.broadcasted_iota(jnp.int32, (rows, lanes), 0) + z * rows
            alive = place < counts[i]
            for b in range(n):
                piece = acc_r[part, i * rows:(i + 1) * rows, b * lanes:(b + 1) * lanes]
                res[part, b, i] = jnp.where(alive, piece, F32(0.0))
        for to in others:
            to_band(part, to).start()
        start[part, :, pl.ds(pl.multiple_of(z * rows, rows), rows)] = res[part, z]
        for copy in start_halo(part, z):
            copy.start()

    def spread(part, sources):
        for s in sources:
            got(rows_of(start, part, s), a_r.at[part, s])
            for copy in start_halo(part, s):
                copy.start()

    def load(k, ref, part, i):
        high, low = split(ref[part, i])
        field[k, i, :, :lanes] = high
        field[k, i, :, lanes:] = low

    def fold(r):
        return (r[:basis, :lanes] + r[:basis, lanes:]) + (r[basis:, :lanes] + r[basis:, lanes:])

    def local_slots(ref, part):
        for i in range(elements):
            load(0, ref, part, i)

        def body(i, carry):
            r = jnp.dot(ham_b[i, 0], field[0, i], preferred_element_type=F32)
            r += jnp.dot(ham_b[i, 1], field[0, lax.rem(i + elements - 1, elements)], preferred_element_type=F32)
            r += jnp.dot(ham_b[i, 2], field[0, lax.rem(i + 1, elements)], preferred_element_type=F32)
            acc[part, i] = fold(r)
            return carry

        lax.fori_loop(0, elements, body, 0)

    def halo_slots(lo, hi, part, i):
        load(1, lo, part, i)
        load(2, hi, part, i)
        r = jnp.dot(ham_b[i, 3], field[1, i], preferred_element_type=F32)
        r += jnp.dot(ham_b[i, 4], field[2, i], preferred_element_type=F32)
        return acc[part, i] + fold(r)

    def middle(part):
        for s in range(n):
            got(rows_of(start_lo, part, s), b_r.at[part, s, 0])
            got(rows_of(start_hi, part, s), b_r.at[part, s, 1])
        for i in range(elements):
            mid[part, i] = halo_slots(start_lo, start_hi, part, i)
            for copy in mid_halo(part, i):
                copy.start()

    def finish(part):
        for i in range(elements):
            got(mid_lo.at[part, i], h_r.at[part, i, 0])
            got(mid_hi.at[part, i], h_r.at[part, i, 1])
            total = halo_slots(mid_lo, mid_hi, part, i)
            out[i, :, part * lanes:(part + 1) * lanes] = 2.0 * total - start[part, i]

    def prepare(i):
        square = (basis, basis)
        place = lax.broadcasted_iota(jnp.int32, square, 0)
        scale = jnp.where(place < counts[i], 1.0 / jnp.full(square, width[0], F32), F32(0.0))
        diagonal_part = jnp.where(
            place == lax.broadcasted_iota(jnp.int32, square, 1), center[0], F32(0.0)
        )
        for slot in range(SLOTS):
            entries = ham_v[i, slot]
            if slot == 0:
                entries = entries - diagonal_part
            high, low = split(entries * scale)
            ham_b[i, slot, :basis] = high
            ham_b[i, slot, basis:] = low

    send_own(0)
    send_own(1)
    orb_copy.wait()
    high, low = split(orb_v[...])
    orb_b[:elements * rows] = high
    orb_b[elements * rows:] = low
    rotate(0, z, True)
    gather_first(0)
    ham_copy.wait()
    prepare(0)
    gather_second(0)
    prepare(1)
    gather_first(1)
    gather_third(0)
    rotate(1, z, True)
    rotated(0)
    gather_second(1)
    prepare(2)
    gather_third(1)
    prepare(3)
    rotated(1)
    spread(0, others)
    local_slots(start, 0)
    spread(1, others[:1])
    middle(0)
    spread(1, others[1:])
    local_slots(start, 1)
    middle(1)
    local_slots(mid, 0)
    finish(0)
    local_slots(mid, 1)
    finish(1)

    for part in range(PARTS):
        for i in range(elements):
            for copy in mid_halo(part, i):
                copy.wait_send()
        for s in range(n):
            for copy in start_halo(part, s):
                copy.wait_send()
        for s in others:
            over_z(part, s).wait_send()
            over_x(part, s).wait_send()
            over_y(part, s).wait_send()
            relay_over_y(part, s).wait_send()
            for k in range(4):
                over_core(part, s, k).wait_send()
            to_band(part, s).wait_send()


def shards(orbitals, rotation, counts, hamiltonian, filter_center, filter_width):
    elements, rows, bands = orbitals.shape
    basis = hamiltonian.shape[2]
    depth = rotation.shape[0]
    n = bands // depth
    lanes = depth // PARTS
    own = (PARTS, elements, basis, lanes)
    dma = pltpu.SemaphoreType.DMA
    in_vmem = pl.BlockSpec(memory_space=pltpu.VMEM)
    in_hbm = pl.BlockSpec(memory_space=pltpu.HBM)
    in_smem = pl.BlockSpec(memory_space=pltpu.SMEM)
    flops = 2 * elements * rows * bands * bands * 3 + 2 * 2 * elements * SLOTS * basis * basis * depth * 4
    return pl.pallas_call(
        functools.partial(kernel, n),
        out_shape=jax.ShapeDtypeStruct((elements, basis, depth), F32),
        in_specs=[in_hbm, in_hbm, in_smem, in_smem, in_smem, in_hbm],
        out_specs=in_vmem,
        scratch_shapes=[
            pltpu.VMEM((elements, SLOTS, basis, basis), F32),
            pltpu.VMEM((elements, SLOTS, 2 * basis, basis), BF16),
            pltpu.VMEM((elements * rows, bands), F32),
            pltpu.VMEM((2 * elements * rows, bands), BF16),
            pltpu.VMEM((PARTS, n, depth, n * lanes), F32),
            pltpu.VMEM((PARTS, n, elements, rows, lanes), F32),
            pltpu.VMEM((PARTS, elements * rows, n * lanes), F32),
            pltpu.VMEM(own, F32), pltpu.VMEM(own, F32), pltpu.VMEM(own, F32),
            pltpu.VMEM(own, F32), pltpu.VMEM(own, F32), pltpu.VMEM(own, F32),
            pltpu.VMEM((3, elements, basis, 2 * lanes), BF16),
            pltpu.VMEM(own, F32),
            dma(()), dma(()), dma((PARTS, n)),
            dma((4, PARTS, n)), dma((4, PARTS, n)),
            dma((PARTS, n, 4)), dma((PARTS, n, 4)),
            dma((PARTS, n)), dma((PARTS, n)),
            dma((PARTS, n, 2)), dma((PARTS, n, 2)),
            dma((PARTS, elements, 2)), dma((PARTS, elements, 2)),
        ],
        compiler_params=pltpu.CompilerParams(
            collective_id=0, has_side_effects=True, vmem_limit_bytes=63 * 1024 * 1024
        ),
        cost_estimate=pl.CostEstimate(flops=flops, bytes_accessed=8 * 1024 * 1024, transcendentals=0),
    )(orbitals.reshape(elements * rows, bands), rotation, counts, filter_center, filter_width, hamiltonian)


def solution(mesh):
    fits = mesh.shape["elem"] == GY and mesh.shape["band"] == 4
    return jax.shard_map(
        shards if fits else general_shards,
        mesh=mesh,
        in_specs=(
            P("elem", "band", None),
            P("band", None),
            P("elem"),
            P("elem", None, None, None),
            P(),
            P(),
        ),
        out_specs=P("elem", None, "band"),
        check_vma=False,
    )
```

```python
import functools

import jax
import jax.numpy as jnp
from jax import lax
from jax.experimental import pallas as pl
from jax.experimental.pallas import tpu as pltpu
from jax.sharding import PartitionSpec as P

GY = 8


def neighbour_rows(field, stride, span, wraps):
    size = lax.axis_size("elem")
    behind, ahead = [], []
    for i in range(size):
        place = (i // stride) % span
        base = i - place * stride
        if wraps or place + 1 < span:
            behind.append((i, base + (place + 1) % span * stride))
        if wraps or place > 0:
            ahead.append((i, base + (place + span - 1) % span * stride))
    return lax.ppermute(field, "elem", behind), lax.ppermute(field, "elem", ahead)


def apply_operator(field, hamiltonian, live):
    layers = lax.axis_size("elem") // GY
    others = [field, jnp.roll(field, 1, axis=0), jnp.roll(field, -1, axis=0)]
    others += neighbour_rows(field, 1, GY, True)
    if layers > 1:
        others += neighbour_rows(field, GY, layers, False)
    total = jnp.zeros(field.shape, jnp.float32)
    for slot, other in enumerate(others):
        total = total + jnp.einsum(
            "erc,ecb->erb", hamiltonian[:, slot], other, precision=lax.Precision.HIGH
        )
    return jnp.where(live[:, :, None], total, jnp.float32(0.0))


def general_shards(orbitals, rotation, counts, hamiltonian, filter_center, filter_width):
    elements, rows_here, bands = orbitals.shape
    basis = hamiltonian.shape[2]
    whole_rotation = lax.all_gather(rotation, "band", axis=0, tiled=True)
    rotated = jnp.einsum(
        "eik,kb->eib", orbitals, whole_rotation, precision=lax.Precision.HIGH
    )
    start = lax.all_to_all(rotated, "band", split_axis=2, concat_axis=1, tiled=True)
    live = jnp.arange(basis, dtype=jnp.int32)[None, :] < counts[:, None]
    start = jnp.where(live[:, :, None], start, jnp.float32(0.0))
    center = filter_center[0]
    width = filter_width[0]
    middle = (apply_operator(start, hamiltonian, live) - center * start) / width
    return 2.0 * (apply_operator(middle, hamiltonian, live) - center * middle) / width - start


F32, BF16 = jnp.float32, jnp.bfloat16
PARTS = 2
SLOTS = 5


def split(x):
    high = x.astype(BF16)
    return high, (x - high.astype(F32)).astype(BF16)


def kernel(
    n, orb, rot, counts, center, width, ham, out,
    ham_v, ham_l, ham_h, orb_v, orb_b, rot_b, rot_s, res, start, start_lo, start_hi, mid, mid_lo, mid_hi,
    field_l, field_h, acc, ham_sem, orb_sem, rot_sem,
    g_s, g_r, c_s, c_r, a_s, a_r, b_s, b_r, h_s, h_r,
):
    e, z = lax.axis_index("elem"), lax.axis_index("band")
    elements, basis = ham.shape[0], ham.shape[2]
    rows = basis // n
    depth = rot.shape[0]
    lanes = start.shape[3]
    share = depth // 8
    x, c = (e // 2) % 2, e % 2
    ahead, behind = lax.rem(e + 1, 8), lax.rem(e + 7, 8)
    beside, across, twin = e + 2 - 4 * x, lax.rem(e + 4, 8), e + 1 - 2 * c
    diagonal = lax.rem(beside + 4, 8)
    planes = (e, beside, across, diagonal)
    others = [z + 1 - 2 * (z // 2), lax.rem(2 + 3 * z, 5), 3 - 3 * (z // 2)]

    def remote(src, dst, send, recv, elem, band):
        return pltpu.make_async_remote_copy(
            src_ref=src, dst_ref=dst, send_sem=send, recv_sem=recv,
            device_id=(elem, band), device_id_type=pl.DeviceIdType.MESH,
        )

    def eighth(part, s, owner):
        return rot_b.at[part, s, pl.ds(pl.multiple_of(owner * share, share), share)]

    def over_z(part, to):
        b = eighth(part, z, e)
        return remote(b, b, g_s.at[0, part, to], g_r.at[0, part, z], e, to)

    def over_x(part, s):
        b = eighth(part, s, e)
        return remote(b, b, g_s.at[1, part, s], g_r.at[1, part, s], beside, z)

    def over_y(part, s):
        b = eighth(part, s, e)
        return remote(b, b, g_s.at[2, part, s], g_r.at[2, part, s], across, z)

    def relay_over_y(part, s):
        b = eighth(part, s, beside)
        return remote(b, b, g_s.at[3, part, s], g_r.at[3, part, s], across, z)

    def relay_over_x(part, s):
        b = eighth(part, s, across)
        return remote(b, b, g_s.at[3, part, s], g_r.at[3, part, s], beside, z)

    def over_core(part, s, k):
        b = eighth(part, s, planes[k])
        return remote(b, b, c_s.at[part, s, k], c_r.at[part, s, k], twin, z)

    def got(dst, recv):
        remote(dst, dst, recv, recv, twin, z).wait_recv()

    def rows_of(ref, part, s):
        return ref.at[part, :, pl.ds(pl.multiple_of(s * rows, rows), rows)]

    def to_band(part, to):
        return remote(res.at[part, to], rows_of(start, part, z), a_s.at[part, to], a_r.at[part, z], e, to)

    def start_halo(part, s):
        b = rows_of(start, part, s)
        return (
            remote(b, rows_of(start_lo, part, s), b_s.at[part, s, 0], b_r.at[part, s, 0], ahead, z),
            remote(b, rows_of(start_hi, part, s), b_s.at[part, s, 1], b_r.at[part, s, 1], behind, z),
        )

    def mid_halo(part, i):
        b = mid.at[part, i]
        return (
            remote(b, mid_lo.at[part, i], h_s.at[part, i, 0], h_r.at[part, i, 0], ahead, z),
            remote(b, mid_hi.at[part, i], h_s.at[part, i, 1], h_r.at[part, i, 1], behind, z),
        )

    barrier = pltpu.get_barrier_semaphore()
    partners = [(ahead, z), (behind, z), (beside, z), (across, z)] + [(e, other) for other in others]
    for elem, band in partners:
        pl.semaphore_signal(barrier, inc=1, device_id=(elem, band), device_id_type=pl.DeviceIdType.MESH)
    ham_copy = pltpu.make_async_copy(ham.at[:, pl.ds(0, SLOTS)], ham_v, ham_sem)
    orb_copy = pltpu.make_async_copy(orb, orb_v, orb_sem)
    rot_copies = [
        pltpu.make_async_copy(
            rot.at[:, pl.ds((b * PARTS + part) * lanes, lanes)],
            rot_b.at[part, z, :, pl.ds(b * lanes, lanes)],
            rot_sem.at[part, b],
        )
        for part in range(PARTS)
        for b in range(n)
    ]
    for copy in rot_copies[:n] + [orb_copy] + rot_copies[n:] + [ham_copy]:
        copy.start()
    pl.semaphore_wait(barrier, len(partners))

    def send_own(part):
        for copy in rot_copies[part * n:(part + 1) * n]:
            copy.wait()
        for to in others:
            over_z(part, to).start()

    def gather_first(part):
        for s in others:
            got(eighth(part, s, e), g_r.at[0, part, s])
            over_x(part, s).start()
            over_y(part, s).start()
            over_core(part, s, 0).start()

    def gather_second(part):
        for s in others:
            got(eighth(part, s, beside), g_r.at[1, part, s])
            got(eighth(part, s, across), g_r.at[2, part, s])

            @pl.when(c == 0)
            def _():
                relay_over_y(part, s).start()

            @pl.when(c == 1)
            def _():
                relay_over_x(part, s).start()

            over_core(part, s, 1).start()
            over_core(part, s, 2).start()

    def gather_third(part):
        for s in others:
            got(eighth(part, s, diagonal), g_r.at[3, part, s])
            over_core(part, s, 3).start()

    def halve(part, j):
        high, low = split(rot_b[part, (z, *others)[j]])
        rot_s[part, 0, j * depth:(j + 1) * depth] = high
        rot_s[part, 1, j * depth:(j + 1) * depth] = low

    def rotated(part):
        for j, s in enumerate(others):
            for k in range(4):
                got(eighth(part, s, planes[k] + 1 - 2 * c), c_r.at[part, s, k])
            halve(part, j + 1)
        for b in range(0, n, 2):
            columns = slice(b * lanes, (b + 2) * lanes)
            both = jnp.dot(orb_b[...], rot_s[part, 0, :, columns], preferred_element_type=F32)
            cross = jnp.dot(orb_b[:elements * rows], rot_s[part, 1, :, columns], preferred_element_type=F32)
            total = both[:elements * rows] + both[elements * rows:] + cross
            for i in range(elements):
                place = lax.broadcasted_iota(jnp.int32, (rows, 2 * lanes), 0) + z * rows
                piece = jnp.where(place < counts[i], total[i * rows:(i + 1) * rows], F32(0.0))
                res[part, b, i] = piece[:, :lanes]
                res[part, b + 1, i] = piece[:, lanes:]
        for to in others:
            to_band(part, to).start()
        start[part, :, pl.ds(pl.multiple_of(z * rows, rows), rows)] = res[part, z]
        for copy in start_halo(part, z):
            copy.start()

    def spread(part):
        for s in others:
            got(rows_of(start, part, s), a_r.at[part, s])
            for copy in start_halo(part, s):
                copy.start()

    def load(ref, part, i, into, first):
        high, low = split(ref[part, i])
        into[first:first + basis, :lanes] = high
        into[first:first + basis, lanes:] = low

    def fold(r):
        return (r[:basis, :lanes] + r[:basis, lanes:]) + (r[basis:, :lanes] + r[basis:, lanes:])

    def local_slots(ref, part):
        for i in range(-1, elements + 1):
            load(ref, part, i % elements, field_l, (i + 1) * basis)
        for i in range(elements):
            around = field_l[i * basis:(i + 3) * basis]
            acc[part, i] = fold(jnp.dot(ham_l[i], around, preferred_element_type=F32))

    def halo_slots(lo, hi, part, i):
        load(lo, part, i, field_h.at[i], 0)
        load(hi, part, i, field_h.at[i], basis)
        return acc[part, i] + fold(jnp.dot(ham_h[i], field_h[i], preferred_element_type=F32))

    def middle(part):
        for s in range(n):
            got(rows_of(start_lo, part, s), b_r.at[part, s, 0])
            got(rows_of(start_hi, part, s), b_r.at[part, s, 1])
        for i in range(elements):
            mid[part, i] = halo_slots(start_lo, start_hi, part, i)
            for copy in mid_halo(part, i):
                copy.start()

    def finish(part):
        for i in range(elements):
            got(mid_lo.at[part, i], h_r.at[part, i, 0])
            got(mid_hi.at[part, i], h_r.at[part, i, 1])
            total = halo_slots(mid_lo, mid_hi, part, i)
            out[i, :, part * lanes:(part + 1) * lanes] = 2.0 * total - start[part, i]

    def prepare(i):
        square = (basis, basis)
        place = lax.broadcasted_iota(jnp.int32, square, 0)
        scale = jnp.where(place < counts[i], 1.0 / jnp.full(square, width[0], F32), F32(0.0))
        diagonal_part = jnp.where(
            place == lax.broadcasted_iota(jnp.int32, square, 1), center[0], F32(0.0)
        )
        own = (ham_v[i, 0] - diagonal_part) * scale
        for into, blocks in (
            (ham_l, [ham_v[i, 1] * scale, own, ham_v[i, 2] * scale]),
            (ham_h, [ham_v[i, 3] * scale, ham_v[i, 4] * scale]),
        ):
            high, low = split(jnp.concatenate(blocks, axis=1))
            into[i, :basis] = high
            into[i, basis:] = low

    send_own(0)
    send_own(1)
    orb_copy.wait()
    for j, s in enumerate((z, *others)):
        high, low = split(orb_v[:, pl.ds(pl.multiple_of(s * depth, depth), depth)])
        orb_b[:elements * rows, j * depth:(j + 1) * depth] = high
        orb_b[elements * rows:, j * depth:(j + 1) * depth] = low
    halve(0, 0)
    halve(1, 0)
    gather_first(0)
    gather_second(0)
    gather_first(1)
    gather_third(0)
    gather_second(1)
    rotated(0)
    gather_third(1)
    rotated(1)
    spread(0)
    ham_copy.wait()
    for i in range(elements):
        prepare(i)
    local_slots(start, 0)
    spread(1)
    middle(0)
    local_slots(start, 1)
    middle(1)
    local_slots(mid, 0)
    finish(0)
    local_slots(mid, 1)
    finish(1)

    for part in range(PARTS):
        for i in range(elements):
            for copy in mid_halo(part, i):
                copy.wait_send()
        for s in range(n):
            for copy in start_halo(part, s):
                copy.wait_send()
        for s in others:
            over_z(part, s).wait_send()
            over_x(part, s).wait_send()
            over_y(part, s).wait_send()
            relay_over_y(part, s).wait_send()
            for k in range(4):
                over_core(part, s, k).wait_send()
            to_band(part, s).wait_send()


def shards(orbitals, rotation, counts, hamiltonian, filter_center, filter_width):
    elements, rows, bands = orbitals.shape
    basis = hamiltonian.shape[2]
    depth = rotation.shape[0]
    n = bands // depth
    lanes = depth // PARTS
    own = (PARTS, elements, basis, lanes)
    dma = pltpu.SemaphoreType.DMA
    in_vmem = pl.BlockSpec(memory_space=pltpu.VMEM)
    in_hbm = pl.BlockSpec(memory_space=pltpu.HBM)
    in_smem = pl.BlockSpec(memory_space=pltpu.SMEM)
    flops = 2 * elements * rows * bands * bands * 3 + 2 * 2 * elements * SLOTS * basis * basis * depth * 4
    return pl.pallas_call(
        functools.partial(kernel, n),
        out_shape=jax.ShapeDtypeStruct((elements, basis, depth), F32),
        in_specs=[in_hbm, in_hbm, in_smem, in_smem, in_smem, in_hbm],
        out_specs=in_vmem,
        scratch_shapes=[
            pltpu.VMEM((elements, SLOTS, basis, basis), F32),
            pltpu.VMEM((elements, 2 * basis, 3 * basis), BF16),
            pltpu.VMEM((elements, 2 * basis, 2 * basis), BF16),
            pltpu.VMEM((elements * rows, bands), F32),
            pltpu.VMEM((2 * elements * rows, bands), BF16),
            pltpu.VMEM((PARTS, n, depth, n * lanes), F32),
            pltpu.VMEM((PARTS, 2, bands, n * lanes), BF16),
            pltpu.VMEM((PARTS, n, elements, rows, lanes), F32),
            pltpu.VMEM(own, F32), pltpu.VMEM(own, F32), pltpu.VMEM(own, F32),
            pltpu.VMEM(own, F32), pltpu.VMEM(own, F32), pltpu.VMEM(own, F32),
            pltpu.VMEM(((elements + 2) * basis, 2 * lanes), BF16),
            pltpu.VMEM((elements, 2 * basis, 2 * lanes), BF16),
            pltpu.VMEM(own, F32),
            dma(()), dma(()), dma((PARTS, n)),
            dma((4, PARTS, n)), dma((4, PARTS, n)),
            dma((PARTS, n, 4)), dma((PARTS, n, 4)),
            dma((PARTS, n)), dma((PARTS, n)),
            dma((PARTS, n, 2)), dma((PARTS, n, 2)),
            dma((PARTS, elements, 2)), dma((PARTS, elements, 2)),
        ],
        compiler_params=pltpu.CompilerParams(
            collective_id=0, has_side_effects=True, vmem_limit_bytes=63 * 1024 * 1024
        ),
        cost_estimate=pl.CostEstimate(flops=flops, bytes_accessed=8 * 1024 * 1024, transcendentals=0),
    )(orbitals.reshape(elements * rows, bands), rotation, counts, filter_center, filter_width, hamiltonian)


def solution(mesh):
    fits = mesh.shape["elem"] == GY and mesh.shape["band"] == 4
    return jax.shard_map(
        shards if fits else general_shards,
        mesh=mesh,
        in_specs=(
            P("elem", "band", None),
            P("band", None),
            P("elem"),
            P("elem", None, None, None),
            P(),
            P(),
        ),
        out_specs=P("elem", None, "band"),
        check_vma=False,
    )
```

```python
import functools

import jax
import jax.numpy as jnp
from jax import lax
from jax.experimental import pallas as pl
from jax.experimental.pallas import tpu as pltpu
from jax.sharding import PartitionSpec as P

GY = 8


def neighbour_rows(field, stride, span, wraps):
    size = lax.axis_size("elem")
    behind, ahead = [], []
    for i in range(size):
        place = (i // stride) % span
        base = i - place * stride
        if wraps or place + 1 < span:
            behind.append((i, base + (place + 1) % span * stride))
        if wraps or place > 0:
            ahead.append((i, base + (place + span - 1) % span * stride))
    return lax.ppermute(field, "elem", behind), lax.ppermute(field, "elem", ahead)


def apply_operator(field, hamiltonian, live):
    layers = lax.axis_size("elem") // GY
    others = [field, jnp.roll(field, 1, axis=0), jnp.roll(field, -1, axis=0)]
    others += neighbour_rows(field, 1, GY, True)
    if layers > 1:
        others += neighbour_rows(field, GY, layers, False)
    total = jnp.zeros(field.shape, jnp.float32)
    for slot, other in enumerate(others):
        total = total + jnp.einsum(
            "erc,ecb->erb", hamiltonian[:, slot], other, precision=lax.Precision.HIGH
        )
    return jnp.where(live[:, :, None], total, jnp.float32(0.0))


def general_shards(orbitals, rotation, counts, hamiltonian, filter_center, filter_width):
    elements, rows_here, bands = orbitals.shape
    basis = hamiltonian.shape[2]
    whole_rotation = lax.all_gather(rotation, "band", axis=0, tiled=True)
    rotated = jnp.einsum(
        "eik,kb->eib", orbitals, whole_rotation, precision=lax.Precision.HIGH
    )
    start = lax.all_to_all(rotated, "band", split_axis=2, concat_axis=1, tiled=True)
    live = jnp.arange(basis, dtype=jnp.int32)[None, :] < counts[:, None]
    start = jnp.where(live[:, :, None], start, jnp.float32(0.0))
    center = filter_center[0]
    width = filter_width[0]
    middle = (apply_operator(start, hamiltonian, live) - center * start) / width
    return 2.0 * (apply_operator(middle, hamiltonian, live) - center * middle) / width - start


F32, BF16 = jnp.float32, jnp.bfloat16
PARTS = 2
SLOTS = 5


def split(x):
    high = x.astype(BF16)
    return high, (x - high.astype(F32)).astype(BF16)


def kernel(
    n, orb, rot, counts, center, width, ham, out,
    ham_v, ham_l, ham_h, orb_v, orb_b, rot_b, rot_s, res, start, start_lo, start_hi, mid, mid_lo, mid_hi,
    field_l, field_h, acc, ham_sem, orb_sem, rot_sem,
    g_s, g_r, c_s, c_r, a_s, a_r, b_s, b_r, h_s, h_r,
):
    e, z = lax.axis_index("elem"), lax.axis_index("band")
    elements, basis = ham.shape[0], ham.shape[2]
    rows = basis // n
    depth = rot.shape[0]
    lanes = start.shape[3]
    share = depth // 8
    x, c = (e // 2) % 2, e % 2
    ahead, behind = lax.rem(e + 1, 8), lax.rem(e + 7, 8)
    beside, across, twin = e + 2 - 4 * x, lax.rem(e + 4, 8), e + 1 - 2 * c
    diagonal = lax.rem(beside + 4, 8)
    planes = (e, beside, across, diagonal)
    others = [z + 1 - 2 * (z // 2), lax.rem(2 + 3 * z, 5), 3 - 3 * (z // 2)]

    def remote(src, dst, send, recv, elem, band):
        return pltpu.make_async_remote_copy(
            src_ref=src, dst_ref=dst, send_sem=send, recv_sem=recv,
            device_id=(elem, band), device_id_type=pl.DeviceIdType.MESH,
        )

    def eighth(part, s, owner):
        return rot_b.at[part, s, pl.ds(pl.multiple_of(owner * share, share), share)]

    def over_z(part, to):
        b = eighth(part, z, e)
        return remote(b, b, g_s.at[0, part, to], g_r.at[0, part, z], e, to)

    def over_x(part, s):
        b = eighth(part, s, e)
        return remote(b, b, g_s.at[1, part, s], g_r.at[1, part, s], beside, z)

    def over_y(part, s):
        b = eighth(part, s, e)
        return remote(b, b, g_s.at[2, part, s], g_r.at[2, part, s], across, z)

    def relay_over_y(part, s):
        b = eighth(part, s, beside)
        return remote(b, b, g_s.at[3, part, s], g_r.at[3, part, s], across, z)

    def relay_over_x(part, s):
        b = eighth(part, s, across)
        return remote(b, b, g_s.at[3, part, s], g_r.at[3, part, s], beside, z)

    def over_core(part, s, k):
        b = eighth(part, s, planes[k])
        return remote(b, b, c_s.at[part, s, k], c_r.at[part, s, k], twin, z)

    def got(dst, recv):
        remote(dst, dst, recv, recv, twin, z).wait_recv()

    def rows_of(ref, part, s):
        return ref.at[part, :, pl.ds(pl.multiple_of(s * rows, rows), rows)]

    def to_band(part, to):
        return remote(res.at[part, to], rows_of(start, part, z), a_s.at[part, to], a_r.at[part, z], e, to)

    def start_halo(part, s):
        b = rows_of(start, part, s)
        return (
            remote(b, rows_of(start_lo, part, s), b_s.at[part, s, 0], b_r.at[part, s, 0], ahead, z),
            remote(b, rows_of(start_hi, part, s), b_s.at[part, s, 1], b_r.at[part, s, 1], behind, z),
        )

    def mid_halo(part, i):
        b = mid.at[part, i]
        return (
            remote(b, mid_lo.at[part, i], h_s.at[part, i, 0], h_r.at[part, i, 0], ahead, z),
            remote(b, mid_hi.at[part, i], h_s.at[part, i, 1], h_r.at[part, i, 1], behind, z),
        )

    barrier = pltpu.get_barrier_semaphore()
    partners = [(ahead, z), (behind, z), (beside, z), (across, z)] + [(e, other) for other in others]
    for elem, band in partners:
        pl.semaphore_signal(barrier, inc=1, device_id=(elem, band), device_id_type=pl.DeviceIdType.MESH)
    ham_copy = pltpu.make_async_copy(ham.at[:, pl.ds(0, SLOTS)], ham_v, ham_sem)
    orb_copy = pltpu.make_async_copy(orb, orb_v, orb_sem)
    rot_copies = [
        pltpu.make_async_copy(
            rot.at[:, pl.ds((b * PARTS + part) * lanes, lanes)],
            rot_b.at[part, z, :, pl.ds(b * lanes, lanes)],
            rot_sem.at[part, b],
        )
        for part in range(PARTS)
        for b in range(n)
    ]
    for copy in rot_copies[:n] + [orb_copy] + rot_copies[n:] + [ham_copy]:
        copy.start()
    pl.semaphore_wait(barrier, len(partners))

    def send_own(part):
        for copy in rot_copies[part * n:(part + 1) * n]:
            copy.wait()
        for to in others:
            over_z(part, to).start()

    def gather_first(part):
        for s in others:
            got(eighth(part, s, e), g_r.at[0, part, s])
            over_x(part, s).start()
            over_y(part, s).start()
            over_core(part, s, 0).start()

    def gather_second(part):
        for s in others:
            got(eighth(part, s, beside), g_r.at[1, part, s])
            got(eighth(part, s, across), g_r.at[2, part, s])

            @pl.when(c == 0)
            def _():
                relay_over_y(part, s).start()

            @pl.when(c == 1)
            def _():
                relay_over_x(part, s).start()

            over_core(part, s, 1).start()
            over_core(part, s, 2).start()

    def gather_third(part):
        for s in others:
            got(eighth(part, s, diagonal), g_r.at[3, part, s])
            over_core(part, s, 3).start()

    def halve(part, j):
        high, low = split(rot_b[part, (z, *others)[j]])
        rot_s[part, 0, j * depth:(j + 1) * depth] = high
        rot_s[part, 1, j * depth:(j + 1) * depth] = low

    def rotated(part):
        for j, s in enumerate(others):
            for k in range(4):
                got(eighth(part, s, planes[k] + 1 - 2 * c), c_r.at[part, s, k])
            halve(part, j + 1)
        for b in range(0, n, 2):
            columns = slice(b * lanes, (b + 2) * lanes)
            both = jnp.dot(orb_b[...], rot_s[part, 0, :, columns], preferred_element_type=F32)
            cross = jnp.dot(orb_b[:elements * rows], rot_s[part, 1, :, columns], preferred_element_type=F32)
            total = both[:elements * rows] + both[elements * rows:] + cross
            for i in range(elements):
                place = lax.broadcasted_iota(jnp.int32, (rows, 2 * lanes), 0) + z * rows
                piece = jnp.where(place < counts[i], total[i * rows:(i + 1) * rows], F32(0.0))
                res[part, b, i] = piece[:, :lanes]
                res[part, b + 1, i] = piece[:, lanes:]
        for to in others:
            to_band(part, to).start()
        start[part, :, pl.ds(pl.multiple_of(z * rows, rows), rows)] = res[part, z]
        for copy in start_halo(part, z):
            copy.start()

    def spread(part):
        for s in others:
            got(rows_of(start, part, s), a_r.at[part, s])
            for copy in start_halo(part, s):
                copy.start()

    def load(ref, part, i, into, first):
        high, low = split(ref[part, i])
        into[first:first + basis, :lanes] = high
        into[first:first + basis, lanes:] = low

    def fold(r):
        return (r[:basis, :lanes] + r[:basis, lanes:]) + (r[basis:, :lanes] + r[basis:, lanes:])

    def local_slots(ref, part):
        for i in range(-1, elements + 1):
            load(ref, part, i % elements, field_l, (i + 1) * basis)
        for i in range(elements):
            around = field_l[i * basis:(i + 3) * basis]
            acc[part, i] = fold(jnp.dot(ham_l[i], around, preferred_element_type=F32))

    def halo_slots(lo, hi, part, i):
        load(lo, part, i, field_h.at[i], 0)
        load(hi, part, i, field_h.at[i], basis)
        return acc[part, i] + fold(jnp.dot(ham_h[i], field_h[i], preferred_element_type=F32))

    def middle(part):
        for s in range(n):
            got(rows_of(start_lo, part, s), b_r.at[part, s, 0])
            got(rows_of(start_hi, part, s), b_r.at[part, s, 1])
        for i in range(elements):
            mid[part, i] = halo_slots(start_lo, start_hi, part, i)
            for copy in mid_halo(part, i):
                copy.start()

    def finish(part):
        for i in range(elements):
            got(mid_lo.at[part, i], h_r.at[part, i, 0])
            got(mid_hi.at[part, i], h_r.at[part, i, 1])
            total = halo_slots(mid_lo, mid_hi, part, i)
            out[i, :, part * lanes:(part + 1) * lanes] = 2.0 * total - start[part, i]

    def prepare(i):
        square = (basis, basis)
        place = lax.broadcasted_iota(jnp.int32, square, 0)
        scale = jnp.where(place < counts[i], 1.0 / jnp.full(square, width[0], F32), F32(0.0))
        diagonal_part = jnp.where(
            place == lax.broadcasted_iota(jnp.int32, square, 1), center[0], F32(0.0)
        )
        own = (ham_v[i, 0] - diagonal_part) * scale
        for into, blocks in (
            (ham_l, [ham_v[i, 1] * scale, own, ham_v[i, 2] * scale]),
            (ham_h, [ham_v[i, 3] * scale, ham_v[i, 4] * scale]),
        ):
            high, low = split(jnp.concatenate(blocks, axis=1))
            into[i, :basis] = high
            into[i, basis:] = low

    send_own(0)
    orb_copy.wait()
    for j, s in enumerate((z, *others)):
        high, low = split(orb_v[:, pl.ds(pl.multiple_of(s * depth, depth), depth)])
        orb_b[:elements * rows, j * depth:(j + 1) * depth] = high
        orb_b[elements * rows:, j * depth:(j + 1) * depth] = low
    halve(0, 0)
    gather_first(0)
    send_own(1)
    halve(1, 0)
    gather_second(0)
    gather_first(1)
    gather_third(0)
    gather_second(1)
    rotated(0)
    gather_third(1)
    rotated(1)
    spread(0)
    ham_copy.wait()
    for i in range(elements):
        prepare(i)
    local_slots(start, 0)
    spread(1)
    middle(0)
    local_slots(start, 1)
    middle(1)
    local_slots(mid, 0)
    finish(0)
    local_slots(mid, 1)
    finish(1)

    for part in range(PARTS):
        for i in range(elements):
            for copy in mid_halo(part, i):
                copy.wait_send()
        for s in range(n):
            for copy in start_halo(part, s):
                copy.wait_send()
        for s in others:
            over_z(part, s).wait_send()
            over_x(part, s).wait_send()
            over_y(part, s).wait_send()
            relay_over_y(part, s).wait_send()
            for k in range(4):
                over_core(part, s, k).wait_send()
            to_band(part, s).wait_send()


def shards(orbitals, rotation, counts, hamiltonian, filter_center, filter_width):
    elements, rows, bands = orbitals.shape
    basis = hamiltonian.shape[2]
    depth = rotation.shape[0]
    n = bands // depth
    lanes = depth // PARTS
    own = (PARTS, elements, basis, lanes)
    dma = pltpu.SemaphoreType.DMA
    in_vmem = pl.BlockSpec(memory_space=pltpu.VMEM)
    in_hbm = pl.BlockSpec(memory_space=pltpu.HBM)
    in_smem = pl.BlockSpec(memory_space=pltpu.SMEM)
    flops = 2 * elements * rows * bands * bands * 3 + 2 * 2 * elements * SLOTS * basis * basis * depth * 4
    return pl.pallas_call(
        functools.partial(kernel, n),
        out_shape=jax.ShapeDtypeStruct((elements, basis, depth), F32),
        in_specs=[in_hbm, in_hbm, in_smem, in_smem, in_smem, in_hbm],
        out_specs=in_vmem,
        scratch_shapes=[
            pltpu.VMEM((elements, SLOTS, basis, basis), F32),
            pltpu.VMEM((elements, 2 * basis, 3 * basis), BF16),
            pltpu.VMEM((elements, 2 * basis, 2 * basis), BF16),
            pltpu.VMEM((elements * rows, bands), F32),
            pltpu.VMEM((2 * elements * rows, bands), BF16),
            pltpu.VMEM((PARTS, n, depth, n * lanes), F32),
            pltpu.VMEM((PARTS, 2, bands, n * lanes), BF16),
            pltpu.VMEM((PARTS, n, elements, rows, lanes), F32),
            pltpu.VMEM(own, F32), pltpu.VMEM(own, F32), pltpu.VMEM(own, F32),
            pltpu.VMEM(own, F32), pltpu.VMEM(own, F32), pltpu.VMEM(own, F32),
            pltpu.VMEM(((elements + 2) * basis, 2 * lanes), BF16),
            pltpu.VMEM((elements, 2 * basis, 2 * lanes), BF16),
            pltpu.VMEM(own, F32),
            dma(()), dma(()), dma((PARTS, n)),
            dma((4, PARTS, n)), dma((4, PARTS, n)),
            dma((PARTS, n, 4)), dma((PARTS, n, 4)),
            dma((PARTS, n)), dma((PARTS, n)),
            dma((PARTS, n, 2)), dma((PARTS, n, 2)),
            dma((PARTS, elements, 2)), dma((PARTS, elements, 2)),
        ],
        compiler_params=pltpu.CompilerParams(
            collective_id=0, has_side_effects=True, vmem_limit_bytes=63 * 1024 * 1024
        ),
        cost_estimate=pl.CostEstimate(flops=flops, bytes_accessed=8 * 1024 * 1024, transcendentals=0),
    )(orbitals.reshape(elements * rows, bands), rotation, counts, filter_center, filter_width, hamiltonian)


def solution(mesh):
    fits = mesh.shape["elem"] == GY and mesh.shape["band"] == 4
    return jax.shard_map(
        shards if fits else general_shards,
        mesh=mesh,
        in_specs=(
            P("elem", "band", None),
            P("band", None),
            P("elem"),
            P("elem", None, None, None),
            P(),
            P(),
        ),
        out_specs=P("elem", None, "band"),
        check_vma=False,
    )
```

```python
import functools

import jax
import jax.numpy as jnp
from jax import lax
from jax.experimental import pallas as pl
from jax.experimental.pallas import tpu as pltpu
from jax.sharding import PartitionSpec as P

GY = 8


def neighbour_rows(field, stride, span, wraps):
    size = lax.axis_size("elem")
    behind, ahead = [], []
    for i in range(size):
        place = (i // stride) % span
        base = i - place * stride
        if wraps or place + 1 < span:
            behind.append((i, base + (place + 1) % span * stride))
        if wraps or place > 0:
            ahead.append((i, base + (place + span - 1) % span * stride))
    return lax.ppermute(field, "elem", behind), lax.ppermute(field, "elem", ahead)


def apply_operator(field, hamiltonian, live):
    layers = lax.axis_size("elem") // GY
    others = [field, jnp.roll(field, 1, axis=0), jnp.roll(field, -1, axis=0)]
    others += neighbour_rows(field, 1, GY, True)
    if layers > 1:
        others += neighbour_rows(field, GY, layers, False)
    total = jnp.zeros(field.shape, jnp.float32)
    for slot, other in enumerate(others):
        total = total + jnp.einsum(
            "erc,ecb->erb", hamiltonian[:, slot], other, precision=lax.Precision.HIGH
        )
    return jnp.where(live[:, :, None], total, jnp.float32(0.0))


def general_shards(orbitals, rotation, counts, hamiltonian, filter_center, filter_width):
    elements, rows_here, bands = orbitals.shape
    basis = hamiltonian.shape[2]
    whole_rotation = lax.all_gather(rotation, "band", axis=0, tiled=True)
    rotated = jnp.einsum(
        "eik,kb->eib", orbitals, whole_rotation, precision=lax.Precision.HIGH
    )
    start = lax.all_to_all(rotated, "band", split_axis=2, concat_axis=1, tiled=True)
    live = jnp.arange(basis, dtype=jnp.int32)[None, :] < counts[:, None]
    start = jnp.where(live[:, :, None], start, jnp.float32(0.0))
    center = filter_center[0]
    width = filter_width[0]
    middle = (apply_operator(start, hamiltonian, live) - center * start) / width
    return 2.0 * (apply_operator(middle, hamiltonian, live) - center * middle) / width - start


F32, BF16 = jnp.float32, jnp.bfloat16
PARTS = 2
SLOTS = 5


def split(x):
    high = x.astype(BF16)
    return high, (x - high.astype(F32)).astype(BF16)


def kernel(
    n, orb, rot, counts, center, width, ham, out,
    ham_v, ham_l, ham_h, orb_v, orb_b, rot_b, rot_s, res, start, start_lo, start_hi, mid, mid_lo, mid_hi,
    field_l, field_h, acc, ham_sem, orb_sem, rot_sem,
    g_s, g_r, c_s, c_r, a_s, a_r, b_s, b_r, h_s, h_r,
):
    e, z = lax.axis_index("elem"), lax.axis_index("band")
    elements, basis = ham.shape[0], ham.shape[2]
    rows = basis // n
    depth = rot.shape[0]
    lanes = start.shape[3]
    share = depth // 8
    x, c = (e // 2) % 2, e % 2
    ahead, behind = lax.rem(e + 1, 8), lax.rem(e + 7, 8)
    beside, across, twin = e + 2 - 4 * x, lax.rem(e + 4, 8), e + 1 - 2 * c
    diagonal = lax.rem(beside + 4, 8)
    planes = (e, beside, across, diagonal)
    others = [z + 1 - 2 * (z // 2), lax.rem(2 + 3 * z, 5), 3 - 3 * (z // 2)]

    def remote(src, dst, send, recv, elem, band):
        return pltpu.make_async_remote_copy(
            src_ref=src, dst_ref=dst, send_sem=send, recv_sem=recv,
            device_id=(elem, band), device_id_type=pl.DeviceIdType.MESH,
        )

    def eighth(part, s, owner):
        return rot_b.at[part, s, pl.ds(pl.multiple_of(owner * share, share), share)]

    def over_z(part, to):
        b = eighth(part, z, e)
        return remote(b, b, g_s.at[0, part, to], g_r.at[0, part, z], e, to)

    def over_x(part, s):
        b = eighth(part, s, e)
        return remote(b, b, g_s.at[1, part, s], g_r.at[1, part, s], beside, z)

    def over_y(part, s):
        b = eighth(part, s, e)
        return remote(b, b, g_s.at[2, part, s], g_r.at[2, part, s], across, z)

    def relay_over_y(part, s):
        b = eighth(part, s, beside)
        return remote(b, b, g_s.at[3, part, s], g_r.at[3, part, s], across, z)

    def relay_over_x(part, s):
        b = eighth(part, s, across)
        return remote(b, b, g_s.at[3, part, s], g_r.at[3, part, s], beside, z)

    def over_core(part, s, k):
        b = eighth(part, s, planes[k])
        return remote(b, b, c_s.at[part, s, k], c_r.at[part, s, k], twin, z)

    def got(dst, recv):
        remote(dst, dst, recv, recv, twin, z).wait_recv()

    def rows_of(ref, part, s):
        return ref.at[part, :, pl.ds(pl.multiple_of(s * rows, rows), rows)]

    def to_band(part, to):
        return remote(res.at[part, to], rows_of(start, part, z), a_s.at[part, to], a_r.at[part, z], e, to)

    def start_halo(part, s):
        b = rows_of(start, part, s)
        return (
            remote(b, rows_of(start_lo, part, s), b_s.at[part, s, 0], b_r.at[part, s, 0], ahead, z),
            remote(b, rows_of(start_hi, part, s), b_s.at[part, s, 1], b_r.at[part, s, 1], behind, z),
        )

    def mid_halo(part, i):
        b = mid.at[part, i]
        return (
            remote(b, mid_lo.at[part, i], h_s.at[part, i, 0], h_r.at[part, i, 0], ahead, z),
            remote(b, mid_hi.at[part, i], h_s.at[part, i, 1], h_r.at[part, i, 1], behind, z),
        )

    barrier = pltpu.get_barrier_semaphore()
    partners = [(ahead, z), (behind, z), (beside, z), (across, z)] + [(e, other) for other in others]
    for elem, band in partners:
        pl.semaphore_signal(barrier, inc=1, device_id=(elem, band), device_id_type=pl.DeviceIdType.MESH)
    ham_copy = pltpu.make_async_copy(ham.at[:, pl.ds(0, SLOTS)], ham_v, ham_sem)
    orb_copy = pltpu.make_async_copy(orb, orb_v, orb_sem)
    rot_copies = [
        pltpu.make_async_copy(
            rot.at[:, pl.ds((b * PARTS + part) * lanes, lanes)],
            rot_b.at[part, z, :, pl.ds(b * lanes, lanes)],
            rot_sem.at[part, b],
        )
        for part in range(PARTS)
        for b in range(n)
    ]
    for copy in rot_copies[:n] + [orb_copy] + rot_copies[n:] + [ham_copy]:
        copy.start()
    pl.semaphore_wait(barrier, len(partners))

    def send_own(part):
        for copy in rot_copies[part * n:(part + 1) * n]:
            copy.wait()
        for to in others:
            over_z(part, to).start()

    def gather_first(part):
        for s in others:
            got(eighth(part, s, e), g_r.at[0, part, s])
            over_x(part, s).start()
            over_y(part, s).start()
            over_core(part, s, 0).start()

    def gather_second(part):
        for s in others:
            got(eighth(part, s, beside), g_r.at[1, part, s])
            got(eighth(part, s, across), g_r.at[2, part, s])

            @pl.when(c == 0)
            def _():
                relay_over_y(part, s).start()

            @pl.when(c == 1)
            def _():
                relay_over_x(part, s).start()

            over_core(part, s, 1).start()
            over_core(part, s, 2).start()

    def gather_third(part):
        for s in others:
            got(eighth(part, s, diagonal), g_r.at[3, part, s])
            over_core(part, s, 3).start()

    def halve(part, j):
        high, low = split(rot_b[part, (z, *others)[j]])
        rot_s[part, 0, j * depth:(j + 1) * depth] = high
        rot_s[part, 1, j * depth:(j + 1) * depth] = low

    def rotated(part):
        for j, s in enumerate(others):
            for k in range(4):
                got(eighth(part, s, planes[k] + 1 - 2 * c), c_r.at[part, s, k])
            halve(part, j + 1)
        for b in range(0, n, 2):
            columns = slice(b * lanes, (b + 2) * lanes)
            both = jnp.dot(orb_b[...], rot_s[part, 0, :, columns], preferred_element_type=F32)
            cross = jnp.dot(orb_b[:elements * rows], rot_s[part, 1, :, columns], preferred_element_type=F32)
            total = both[:elements * rows] + both[elements * rows:] + cross
            for i in range(elements):
                place = lax.broadcasted_iota(jnp.int32, (rows, 2 * lanes), 0) + z * rows
                piece = jnp.where(place < counts[i], total[i * rows:(i + 1) * rows], F32(0.0))
                res[part, b, i] = piece[:, :lanes]
                res[part, b + 1, i] = piece[:, lanes:]
        for to in others:
            to_band(part, to).start()
        start[part, :, pl.ds(pl.multiple_of(z * rows, rows), rows)] = res[part, z]
        for copy in start_halo(part, z):
            copy.start()

    def spread(part, sources):
        for s in sources:
            got(rows_of(start, part, s), a_r.at[part, s])
            for copy in start_halo(part, s):
                copy.start()

    def load(ref, part, i, into, first):
        high, low = split(ref[part, i])
        into[first:first + basis, :lanes] = high
        into[first:first + basis, lanes:] = low

    def fold(r):
        return (r[:basis, :lanes] + r[:basis, lanes:]) + (r[basis:, :lanes] + r[basis:, lanes:])

    def local_slots(ref, part):
        for i in range(-1, elements + 1):
            load(ref, part, i % elements, field_l, (i + 1) * basis)
        for i in range(elements):
            around = field_l[i * basis:(i + 3) * basis]
            acc[part, i] = fold(jnp.dot(ham_l[i], around, preferred_element_type=F32))

    def halo_slots(lo, hi, part, i):
        load(lo, part, i, field_h.at[i], 0)
        load(hi, part, i, field_h.at[i], basis)
        return acc[part, i] + fold(jnp.dot(ham_h[i], field_h[i], preferred_element_type=F32))

    def middle(part):
        for s in range(n):
            got(rows_of(start_lo, part, s), b_r.at[part, s, 0])
            got(rows_of(start_hi, part, s), b_r.at[part, s, 1])
        for i in range(elements):
            mid[part, i] = halo_slots(start_lo, start_hi, part, i)
            for copy in mid_halo(part, i):
                copy.start()

    def finish(part):
        for i in range(elements):
            got(mid_lo.at[part, i], h_r.at[part, i, 0])
            got(mid_hi.at[part, i], h_r.at[part, i, 1])
            total = halo_slots(mid_lo, mid_hi, part, i)
            out[i, :, part * lanes:(part + 1) * lanes] = 2.0 * total - start[part, i]

    def prepare(i):
        square = (basis, basis)
        place = lax.broadcasted_iota(jnp.int32, square, 0)
        scale = jnp.where(place < counts[i], 1.0 / jnp.full(square, width[0], F32), F32(0.0))
        diagonal_part = jnp.where(
            place == lax.broadcasted_iota(jnp.int32, square, 1), center[0], F32(0.0)
        )
        own = (ham_v[i, 0] - diagonal_part) * scale
        for into, blocks in (
            (ham_l, [ham_v[i, 1] * scale, own, ham_v[i, 2] * scale]),
            (ham_h, [ham_v[i, 3] * scale, ham_v[i, 4] * scale]),
        ):
            high, low = split(jnp.concatenate(blocks, axis=1))
            into[i, :basis] = high
            into[i, basis:] = low

    send_own(0)
    orb_copy.wait()
    for j, s in enumerate((z, *others)):
        high, low = split(orb_v[:, pl.ds(pl.multiple_of(s * depth, depth), depth)])
        orb_b[:elements * rows, j * depth:(j + 1) * depth] = high
        orb_b[elements * rows:, j * depth:(j + 1) * depth] = low
    halve(0, 0)
    gather_first(0)
    send_own(1)
    halve(1, 0)
    ham_copy.wait()
    prepare(0)
    gather_second(0)
    prepare(1)
    gather_third(0)
    prepare(2)
    gather_first(1)
    rotated(0)
    gather_second(1)
    prepare(3)
    gather_third(1)
    rotated(1)
    spread(0, others)
    local_slots(start, 0)
    spread(1, others[:1])
    middle(0)
    spread(1, others[1:])
    local_slots(start, 1)
    middle(1)
    local_slots(mid, 0)
    finish(0)
    local_slots(mid, 1)
    finish(1)

    for part in range(PARTS):
        for i in range(elements):
            for copy in mid_halo(part, i):
                copy.wait_send()
        for s in range(n):
            for copy in start_halo(part, s):
                copy.wait_send()
        for s in others:
            over_z(part, s).wait_send()
            over_x(part, s).wait_send()
            over_y(part, s).wait_send()
            relay_over_y(part, s).wait_send()
            for k in range(4):
                over_core(part, s, k).wait_send()
            to_band(part, s).wait_send()


def shards(orbitals, rotation, counts, hamiltonian, filter_center, filter_width):
    elements, rows, bands = orbitals.shape
    basis = hamiltonian.shape[2]
    depth = rotation.shape[0]
    n = bands // depth
    lanes = depth // PARTS
    own = (PARTS, elements, basis, lanes)
    dma = pltpu.SemaphoreType.DMA
    in_vmem = pl.BlockSpec(memory_space=pltpu.VMEM)
    in_hbm = pl.BlockSpec(memory_space=pltpu.HBM)
    in_smem = pl.BlockSpec(memory_space=pltpu.SMEM)
    flops = 2 * elements * rows * bands * bands * 3 + 2 * 2 * elements * SLOTS * basis * basis * depth * 4
    return pl.pallas_call(
        functools.partial(kernel, n),
        out_shape=jax.ShapeDtypeStruct((elements, basis, depth), F32),
        in_specs=[in_hbm, in_hbm, in_smem, in_smem, in_smem, in_hbm],
        out_specs=in_vmem,
        scratch_shapes=[
            pltpu.VMEM((elements, SLOTS, basis, basis), F32),
            pltpu.VMEM((elements, 2 * basis, 3 * basis), BF16),
            pltpu.VMEM((elements, 2 * basis, 2 * basis), BF16),
            pltpu.VMEM((elements * rows, bands), F32),
            pltpu.VMEM((2 * elements * rows, bands), BF16),
            pltpu.VMEM((PARTS, n, depth, n * lanes), F32),
            pltpu.VMEM((PARTS, 2, bands, n * lanes), BF16),
            pltpu.VMEM((PARTS, n, elements, rows, lanes), F32),
            pltpu.VMEM(own, F32), pltpu.VMEM(own, F32), pltpu.VMEM(own, F32),
            pltpu.VMEM(own, F32), pltpu.VMEM(own, F32), pltpu.VMEM(own, F32),
            pltpu.VMEM(((elements + 2) * basis, 2 * lanes), BF16),
            pltpu.VMEM((elements, 2 * basis, 2 * lanes), BF16),
            pltpu.VMEM(own, F32),
            dma(()), dma(()), dma((PARTS, n)),
            dma((4, PARTS, n)), dma((4, PARTS, n)),
            dma((PARTS, n, 4)), dma((PARTS, n, 4)),
            dma((PARTS, n)), dma((PARTS, n)),
            dma((PARTS, n, 2)), dma((PARTS, n, 2)),
            dma((PARTS, elements, 2)), dma((PARTS, elements, 2)),
        ],
        compiler_params=pltpu.CompilerParams(
            collective_id=0, has_side_effects=True, vmem_limit_bytes=63 * 1024 * 1024
        ),
        cost_estimate=pl.CostEstimate(flops=flops, bytes_accessed=8 * 1024 * 1024, transcendentals=0),
    )(orbitals.reshape(elements * rows, bands), rotation, counts, filter_center, filter_width, hamiltonian)


def solution(mesh):
    fits = mesh.shape["elem"] == GY and mesh.shape["band"] == 4
    return jax.shard_map(
        shards if fits else general_shards,
        mesh=mesh,
        in_specs=(
            P("elem", "band", None),
            P("band", None),
            P("elem"),
            P("elem", None, None, None),
            P(),
            P(),
        ),
        out_specs=P("elem", None, "band"),
        check_vma=False,
    )
```

```python
import functools

import jax
import jax.numpy as jnp
from jax import lax
from jax.experimental import pallas as pl
from jax.experimental.pallas import tpu as pltpu
from jax.sharding import PartitionSpec as P

GY = 8


def neighbour_rows(field, stride, span, wraps):
    size = lax.axis_size("elem")
    behind, ahead = [], []
    for i in range(size):
        place = (i // stride) % span
        base = i - place * stride
        if wraps or place + 1 < span:
            behind.append((i, base + (place + 1) % span * stride))
        if wraps or place > 0:
            ahead.append((i, base + (place + span - 1) % span * stride))
    return lax.ppermute(field, "elem", behind), lax.ppermute(field, "elem", ahead)


def apply_operator(field, hamiltonian, live):
    layers = lax.axis_size("elem") // GY
    others = [field, jnp.roll(field, 1, axis=0), jnp.roll(field, -1, axis=0)]
    others += neighbour_rows(field, 1, GY, True)
    if layers > 1:
        others += neighbour_rows(field, GY, layers, False)
    total = jnp.zeros(field.shape, jnp.float32)
    for slot, other in enumerate(others):
        total = total + jnp.einsum(
            "erc,ecb->erb", hamiltonian[:, slot], other, precision=lax.Precision.HIGH
        )
    return jnp.where(live[:, :, None], total, jnp.float32(0.0))


def general_shards(orbitals, rotation, counts, hamiltonian, filter_center, filter_width):
    elements, rows_here, bands = orbitals.shape
    basis = hamiltonian.shape[2]
    whole_rotation = lax.all_gather(rotation, "band", axis=0, tiled=True)
    rotated = jnp.einsum(
        "eik,kb->eib", orbitals, whole_rotation, precision=lax.Precision.HIGH
    )
    start = lax.all_to_all(rotated, "band", split_axis=2, concat_axis=1, tiled=True)
    live = jnp.arange(basis, dtype=jnp.int32)[None, :] < counts[:, None]
    start = jnp.where(live[:, :, None], start, jnp.float32(0.0))
    center = filter_center[0]
    width = filter_width[0]
    middle = (apply_operator(start, hamiltonian, live) - center * start) / width
    return 2.0 * (apply_operator(middle, hamiltonian, live) - center * middle) / width - start


F32, BF16 = jnp.float32, jnp.bfloat16
PARTS = 2
SLOTS = 5


def split(x):
    high = x.astype(BF16)
    return high, (x - high.astype(F32)).astype(BF16)


def kernel(
    n, orb, rot, counts, center, width, ham, out,
    ham_v, ham_l, ham_h, orb_v, orb_b, rot_b, rot_s, res, start, start_lo, start_hi, mid, mid_lo, mid_hi,
    field_l, field_h, acc, ham_sem, orb_sem, rot_sem,
    g_s, g_r, c_s, c_r, a_s, a_r, b_s, b_r, h_s, h_r,
):
    e, z = lax.axis_index("elem"), lax.axis_index("band")
    elements, basis = ham.shape[0], ham.shape[2]
    rows = basis // n
    depth = rot.shape[0]
    lanes = start.shape[3]
    share = depth // 8
    x, c = (e // 2) % 2, e % 2
    ahead, behind = lax.rem(e + 1, 8), lax.rem(e + 7, 8)
    beside, across, twin = e + 2 - 4 * x, lax.rem(e + 4, 8), e + 1 - 2 * c
    diagonal = lax.rem(beside + 4, 8)
    planes = (e, beside, across, diagonal)
    others = [z + 1 - 2 * (z // 2), lax.rem(2 + 3 * z, 5), 3 - 3 * (z // 2)]

    def remote(src, dst, send, recv, elem, band):
        return pltpu.make_async_remote_copy(
            src_ref=src, dst_ref=dst, send_sem=send, recv_sem=recv,
            device_id=(elem, band), device_id_type=pl.DeviceIdType.MESH,
        )

    def eighth(part, s, owner):
        return rot_b.at[part, s, pl.ds(pl.multiple_of(owner * share, share), share)]

    def over_z(part, to):
        b = eighth(part, z, e)
        return remote(b, b, g_s.at[0, part, to], g_r.at[0, part, z], e, to)

    def over_x(part, s):
        b = eighth(part, s, e)
        return remote(b, b, g_s.at[1, part, s], g_r.at[1, part, s], beside, z)

    def over_y(part, s):
        b = eighth(part, s, e)
        return remote(b, b, g_s.at[2, part, s], g_r.at[2, part, s], across, z)

    def relay_over_y(part, s):
        b = eighth(part, s, beside)
        return remote(b, b, g_s.at[3, part, s], g_r.at[3, part, s], across, z)

    def relay_over_x(part, s):
        b = eighth(part, s, across)
        return remote(b, b, g_s.at[3, part, s], g_r.at[3, part, s], beside, z)

    def over_core(part, s, k):
        b = eighth(part, s, planes[k])
        return remote(b, b, c_s.at[part, s, k], c_r.at[part, s, k], twin, z)

    def got(dst, recv):
        remote(dst, dst, recv, recv, twin, z).wait_recv()

    def rows_of(ref, part, s):
        return ref.at[part, :, pl.ds(pl.multiple_of(s * rows, rows), rows)]

    def to_band(part, to):
        return remote(res.at[part, to], rows_of(start, part, z), a_s.at[part, to], a_r.at[part, z], e, to)

    def start_halo(part, s):
        b = rows_of(start, part, s)
        return (
            remote(b, rows_of(start_lo, part, s), b_s.at[part, s, 0], b_r.at[part, s, 0], ahead, z),
            remote(b, rows_of(start_hi, part, s), b_s.at[part, s, 1], b_r.at[part, s, 1], behind, z),
        )

    def mid_halo(part, i):
        b = mid.at[part, i]
        return (
            remote(b, mid_lo.at[part, i], h_s.at[part, i, 0], h_r.at[part, i, 0], ahead, z),
            remote(b, mid_hi.at[part, i], h_s.at[part, i, 1], h_r.at[part, i, 1], behind, z),
        )

    barrier = pltpu.get_barrier_semaphore()
    partners = [(ahead, z), (behind, z), (beside, z), (across, z)] + [(e, other) for other in others]
    for elem, band in partners:
        pl.semaphore_signal(barrier, inc=1, device_id=(elem, band), device_id_type=pl.DeviceIdType.MESH)
    ham_copy = pltpu.make_async_copy(ham.at[:, pl.ds(0, SLOTS)], ham_v, ham_sem)
    orb_copy = pltpu.make_async_copy(orb, orb_v, orb_sem)
    rot_copies = [
        pltpu.make_async_copy(
            rot.at[:, pl.ds((b * PARTS + part) * lanes, lanes)],
            rot_b.at[part, z, :, pl.ds(b * lanes, lanes)],
            rot_sem.at[part, b],
        )
        for part in range(PARTS)
        for b in range(n)
    ]
    for copy in rot_copies[:n] + [orb_copy] + rot_copies[n:] + [ham_copy]:
        copy.start()
    pl.semaphore_wait(barrier, len(partners))

    def send_own(part):
        for copy in rot_copies[part * n:(part + 1) * n]:
            copy.wait()
        for to in others:
            over_z(part, to).start()

    def gather_first(part):
        for s in others:
            got(eighth(part, s, e), g_r.at[0, part, s])
            over_x(part, s).start()
            over_y(part, s).start()
            over_core(part, s, 0).start()

    def gather_second(part):
        for s in others:
            got(eighth(part, s, beside), g_r.at[1, part, s])
            got(eighth(part, s, across), g_r.at[2, part, s])

            @pl.when(c == 0)
            def _():
                relay_over_y(part, s).start()

            @pl.when(c == 1)
            def _():
                relay_over_x(part, s).start()

            over_core(part, s, 1).start()
            over_core(part, s, 2).start()

    def gather_third(part):
        for s in others:
            got(eighth(part, s, diagonal), g_r.at[3, part, s])
            over_core(part, s, 3).start()

    def halve(part, j):
        high, low = split(rot_b[part, (z, *others)[j]])
        rot_s[part, 0, j * depth:(j + 1) * depth] = high
        rot_s[part, 1, j * depth:(j + 1) * depth] = low

    def rotated(part):
        for j, s in enumerate(others):
            for k in range(4):
                got(eighth(part, s, planes[k] + 1 - 2 * c), c_r.at[part, s, k])
            halve(part, j + 1)
        for b in range(0, n, 2):
            columns = slice(b * lanes, (b + 2) * lanes)
            both = jnp.dot(orb_b[...], rot_s[part, 0, :, columns], preferred_element_type=F32)
            cross = jnp.dot(orb_b[:elements * rows], rot_s[part, 1, :, columns], preferred_element_type=F32)
            total = both[:elements * rows] + both[elements * rows:] + cross
            for i in range(elements):
                place = lax.broadcasted_iota(jnp.int32, (rows, 2 * lanes), 0) + z * rows
                piece = jnp.where(place < counts[i], total[i * rows:(i + 1) * rows], F32(0.0))
                res[part, b, i] = piece[:, :lanes]
                res[part, b + 1, i] = piece[:, lanes:]
        for to in others:
            to_band(part, to).start()
        start[part, :, pl.ds(pl.multiple_of(z * rows, rows), rows)] = res[part, z]
        for copy in start_halo(part, z):
            copy.start()

    def spread(part, sources):
        for s in sources:
            got(rows_of(start, part, s), a_r.at[part, s])
            for copy in start_halo(part, s):
                copy.start()

    def load(ref, part, i, into, first):
        high, low = split(ref[part, i])
        into[first:first + basis, :lanes] = high
        into[first:first + basis, lanes:] = low

    def fold(r):
        return (r[:basis, :lanes] + r[:basis, lanes:]) + (r[basis:, :lanes] + r[basis:, lanes:])

    def local_slots(ref, part):
        for i in range(-1, elements + 1):
            load(ref, part, i % elements, field_l, (i + 1) * basis)
        for i in range(elements):
            around = field_l[i * basis:(i + 3) * basis]
            acc[part, i] = fold(jnp.dot(ham_l[i], around, preferred_element_type=F32))

    def halo_slots(lo, hi, part, i):
        load(lo, part, i, field_h.at[i], 0)
        load(hi, part, i, field_h.at[i], basis)
        return acc[part, i] + fold(jnp.dot(ham_h[i], field_h[i], preferred_element_type=F32))

    def middle(part):
        for s in range(n):
            got(rows_of(start_lo, part, s), b_r.at[part, s, 0])
            got(rows_of(start_hi, part, s), b_r.at[part, s, 1])
        for i in range(elements):
            mid[part, i] = halo_slots(start_lo, start_hi, part, i)
            for copy in mid_halo(part, i):
                copy.start()

    def finish(part):
        for i in range(elements):
            got(mid_lo.at[part, i], h_r.at[part, i, 0])
            got(mid_hi.at[part, i], h_r.at[part, i, 1])
            total = halo_slots(mid_lo, mid_hi, part, i)
            out[i, :, part * lanes:(part + 1) * lanes] = 2.0 * total - start[part, i]

    def prepare(i):
        square = (basis, basis)
        place = lax.broadcasted_iota(jnp.int32, square, 0)
        scale = jnp.where(place < counts[i], 1.0 / jnp.full(square, width[0], F32), F32(0.0))
        diagonal_part = jnp.where(
            place == lax.broadcasted_iota(jnp.int32, square, 1), center[0], F32(0.0)
        )
        own = (ham_v[i, 0] - diagonal_part) * scale
        for into, blocks in (
            (ham_l, [ham_v[i, 1] * scale, own, ham_v[i, 2] * scale]),
            (ham_h, [ham_v[i, 3] * scale, ham_v[i, 4] * scale]),
        ):
            high, low = split(jnp.concatenate(blocks, axis=1))
            into[i, :basis] = high
            into[i, basis:] = low

    send_own(0)
    orb_copy.wait()
    for j, s in enumerate((z, *others)):
        high, low = split(orb_v[:, pl.ds(pl.multiple_of(s * depth, depth), depth)])
        orb_b[:elements * rows, j * depth:(j + 1) * depth] = high
        orb_b[elements * rows:, j * depth:(j + 1) * depth] = low
    halve(0, 0)
    gather_first(0)
    send_own(1)
    halve(1, 0)
    gather_second(0)
    gather_third(0)
    gather_first(1)
    gather_second(1)
    rotated(0)
    gather_third(1)
    rotated(1)
    spread(0, others)
    ham_copy.wait()
    prepare(0)
    prepare(1)
    spread(1, others[:1])
    prepare(2)
    prepare(3)
    spread(1, others[1:])
    local_slots(start, 0)
    middle(0)
    local_slots(start, 1)
    middle(1)
    local_slots(mid, 0)
    finish(0)
    local_slots(mid, 1)
    finish(1)

    for part in range(PARTS):
        for i in range(elements):
            for copy in mid_halo(part, i):
                copy.wait_send()
        for s in range(n):
            for copy in start_halo(part, s):
                copy.wait_send()
        for s in others:
            over_z(part, s).wait_send()
            over_x(part, s).wait_send()
            over_y(part, s).wait_send()
            relay_over_y(part, s).wait_send()
            for k in range(4):
                over_core(part, s, k).wait_send()
            to_band(part, s).wait_send()


def shards(orbitals, rotation, counts, hamiltonian, filter_center, filter_width):
    elements, rows, bands = orbitals.shape
    basis = hamiltonian.shape[2]
    depth = rotation.shape[0]
    n = bands // depth
    lanes = depth // PARTS
    own = (PARTS, elements, basis, lanes)
    dma = pltpu.SemaphoreType.DMA
    in_vmem = pl.BlockSpec(memory_space=pltpu.VMEM)
    in_hbm = pl.BlockSpec(memory_space=pltpu.HBM)
    in_smem = pl.BlockSpec(memory_space=pltpu.SMEM)
    flops = 2 * elements * rows * bands * bands * 3 + 2 * 2 * elements * SLOTS * basis * basis * depth * 4
    return pl.pallas_call(
        functools.partial(kernel, n),
        out_shape=jax.ShapeDtypeStruct((elements, basis, depth), F32),
        in_specs=[in_hbm, in_hbm, in_smem, in_smem, in_smem, in_hbm],
        out_specs=in_vmem,
        scratch_shapes=[
            pltpu.VMEM((elements, SLOTS, basis, basis), F32),
            pltpu.VMEM((elements, 2 * basis, 3 * basis), BF16),
            pltpu.VMEM((elements, 2 * basis, 2 * basis), BF16),
            pltpu.VMEM((elements * rows, bands), F32),
            pltpu.VMEM((2 * elements * rows, bands), BF16),
            pltpu.VMEM((PARTS, n, depth, n * lanes), F32),
            pltpu.VMEM((PARTS, 2, bands, n * lanes), BF16),
            pltpu.VMEM((PARTS, n, elements, rows, lanes), F32),
            pltpu.VMEM(own, F32), pltpu.VMEM(own, F32), pltpu.VMEM(own, F32),
            pltpu.VMEM(own, F32), pltpu.VMEM(own, F32), pltpu.VMEM(own, F32),
            pltpu.VMEM(((elements + 2) * basis, 2 * lanes), BF16),
            pltpu.VMEM((elements, 2 * basis, 2 * lanes), BF16),
            pltpu.VMEM(own, F32),
            dma(()), dma(()), dma((PARTS, n)),
            dma((4, PARTS, n)), dma((4, PARTS, n)),
            dma((PARTS, n, 4)), dma((PARTS, n, 4)),
            dma((PARTS, n)), dma((PARTS, n)),
            dma((PARTS, n, 2)), dma((PARTS, n, 2)),
            dma((PARTS, elements, 2)), dma((PARTS, elements, 2)),
        ],
        compiler_params=pltpu.CompilerParams(
            collective_id=0, has_side_effects=True, vmem_limit_bytes=63 * 1024 * 1024
        ),
        cost_estimate=pl.CostEstimate(flops=flops, bytes_accessed=8 * 1024 * 1024, transcendentals=0),
    )(orbitals.reshape(elements * rows, bands), rotation, counts, filter_center, filter_width, hamiltonian)


def solution(mesh):
    fits = mesh.shape["elem"] == GY and mesh.shape["band"] == 4
    return jax.shard_map(
        shards if fits else general_shards,
        mesh=mesh,
        in_specs=(
            P("elem", "band", None),
            P("band", None),
            P("elem"),
            P("elem", None, None, None),
            P(),
            P(),
        ),
        out_specs=P("elem", None, "band"),
        check_vma=False,
    )
```

```python
import functools

import jax
import jax.numpy as jnp
from jax import lax
from jax.experimental import pallas as pl
from jax.experimental.pallas import tpu as pltpu
from jax.sharding import PartitionSpec as P

GY = 8


def neighbour_rows(field, stride, span, wraps):
    size = lax.axis_size("elem")
    behind, ahead = [], []
    for i in range(size):
        place = (i // stride) % span
        base = i - place * stride
        if wraps or place + 1 < span:
            behind.append((i, base + (place + 1) % span * stride))
        if wraps or place > 0:
            ahead.append((i, base + (place + span - 1) % span * stride))
    return lax.ppermute(field, "elem", behind), lax.ppermute(field, "elem", ahead)


def apply_operator(field, hamiltonian, live):
    layers = lax.axis_size("elem") // GY
    others = [field, jnp.roll(field, 1, axis=0), jnp.roll(field, -1, axis=0)]
    others += neighbour_rows(field, 1, GY, True)
    if layers > 1:
        others += neighbour_rows(field, GY, layers, False)
    total = jnp.zeros(field.shape, jnp.float32)
    for slot, other in enumerate(others):
        total = total + jnp.einsum(
            "erc,ecb->erb", hamiltonian[:, slot], other, precision=lax.Precision.HIGH
        )
    return jnp.where(live[:, :, None], total, jnp.float32(0.0))


def general_shards(orbitals, rotation, counts, hamiltonian, filter_center, filter_width):
    elements, rows_here, bands = orbitals.shape
    basis = hamiltonian.shape[2]
    whole_rotation = lax.all_gather(rotation, "band", axis=0, tiled=True)
    rotated = jnp.einsum(
        "eik,kb->eib", orbitals, whole_rotation, precision=lax.Precision.HIGH
    )
    start = lax.all_to_all(rotated, "band", split_axis=2, concat_axis=1, tiled=True)
    live = jnp.arange(basis, dtype=jnp.int32)[None, :] < counts[:, None]
    start = jnp.where(live[:, :, None], start, jnp.float32(0.0))
    center = filter_center[0]
    width = filter_width[0]
    middle = (apply_operator(start, hamiltonian, live) - center * start) / width
    return 2.0 * (apply_operator(middle, hamiltonian, live) - center * middle) / width - start


F32, BF16 = jnp.float32, jnp.bfloat16
PARTS = 2
SLOTS = 5


def split(x):
    high = x.astype(BF16)
    return high, (x - high.astype(F32)).astype(BF16)


def kernel(
    n, orb, rot, counts, center, width, ham, out,
    ham_v, ham_l, ham_h, orb_v, orb_b, rot_b, rot_s, res, start, start_lo, start_hi, mid, mid_lo, mid_hi,
    field_l, field_h, acc, ham_sem, orb_sem, rot_sem,
    g_s, g_r, c_s, c_r, a_s, a_r, b_s, b_r, h_s, h_r,
):
    e, z = lax.axis_index("elem"), lax.axis_index("band")
    elements, basis = ham.shape[0], ham.shape[2]
    rows = basis // n
    depth = rot.shape[0]
    lanes = start.shape[3]
    share = depth // 8
    x, c = (e // 2) % 2, e % 2
    ahead, behind = lax.rem(e + 1, 8), lax.rem(e + 7, 8)
    beside, across, twin = e + 2 - 4 * x, lax.rem(e + 4, 8), e + 1 - 2 * c
    diagonal = lax.rem(beside + 4, 8)
    planes = (e, beside, across, diagonal)
    others = [z + 1 - 2 * (z // 2), lax.rem(2 + 3 * z, 5), 3 - 3 * (z // 2)]

    def remote(src, dst, send, recv, elem, band):
        return pltpu.make_async_remote_copy(
            src_ref=src, dst_ref=dst, send_sem=send, recv_sem=recv,
            device_id=(elem, band), device_id_type=pl.DeviceIdType.MESH,
        )

    def eighth(part, s, owner):
        return rot_b.at[part, s, pl.ds(pl.multiple_of(owner * share, share), share)]

    def over_z(part, to):
        b = eighth(part, z, e)
        return remote(b, b, g_s.at[0, part, to], g_r.at[0, part, z], e, to)

    def over_x(part, s):
        b = eighth(part, s, e)
        return remote(b, b, g_s.at[1, part, s], g_r.at[1, part, s], beside, z)

    def over_y(part, s):
        b = eighth(part, s, e)
        return remote(b, b, g_s.at[2, part, s], g_r.at[2, part, s], across, z)

    def relay_over_y(part, s):
        b = eighth(part, s, beside)
        return remote(b, b, g_s.at[3, part, s], g_r.at[3, part, s], across, z)

    def relay_over_x(part, s):
        b = eighth(part, s, across)
        return remote(b, b, g_s.at[3, part, s], g_r.at[3, part, s], beside, z)

    def over_core(part, s, k):
        b = eighth(part, s, planes[k])
        return remote(b, b, c_s.at[part, s, k], c_r.at[part, s, k], twin, z)

    def got(dst, recv):
        remote(dst, dst, recv, recv, twin, z).wait_recv()

    def rows_of(ref, part, s):
        return ref.at[part, :, pl.ds(pl.multiple_of(s * rows, rows), rows)]

    def to_band(part, to):
        return remote(res.at[part, to], rows_of(start, part, z), a_s.at[part, to], a_r.at[part, z], e, to)

    def start_halo(part, s):
        b = rows_of(start, part, s)
        return (
            remote(b, rows_of(start_lo, part, s), b_s.at[part, s, 0], b_r.at[part, s, 0], ahead, z),
            remote(b, rows_of(start_hi, part, s), b_s.at[part, s, 1], b_r.at[part, s, 1], behind, z),
        )

    def mid_halo(part, i):
        b = mid.at[part, i]
        return (
            remote(b, mid_lo.at[part, i], h_s.at[part, i, 0], h_r.at[part, i, 0], ahead, z),
            remote(b, mid_hi.at[part, i], h_s.at[part, i, 1], h_r.at[part, i, 1], behind, z),
        )

    barrier = pltpu.get_barrier_semaphore()
    partners = [(ahead, z), (behind, z), (beside, z), (across, z)] + [(e, other) for other in others]
    for elem, band in partners:
        pl.semaphore_signal(barrier, inc=1, device_id=(elem, band), device_id_type=pl.DeviceIdType.MESH)
    ham_copy = pltpu.make_async_copy(ham.at[:, pl.ds(0, SLOTS)], ham_v, ham_sem)
    orb_copy = pltpu.make_async_copy(orb, orb_v, orb_sem)
    rot_copies = [
        pltpu.make_async_copy(
            rot.at[:, pl.ds((b * PARTS + part) * lanes, lanes)],
            rot_b.at[part, z, :, pl.ds(b * lanes, lanes)],
            rot_sem.at[part, b],
        )
        for part in range(PARTS)
        for b in range(n)
    ]
    for copy in rot_copies[:n] + [orb_copy] + rot_copies[n:] + [ham_copy]:
        copy.start()
    pl.semaphore_wait(barrier, len(partners))

    def send_own(part):
        for copy in rot_copies[part * n:(part + 1) * n]:
            copy.wait()
        for to in others:
            over_z(part, to).start()

    def gather_first(part):
        for s in others:
            got(eighth(part, s, e), g_r.at[0, part, s])
            over_x(part, s).start()
            over_y(part, s).start()
            over_core(part, s, 0).start()

    def gather_second(part):
        for s in others:
            got(eighth(part, s, beside), g_r.at[1, part, s])
            got(eighth(part, s, across), g_r.at[2, part, s])

            @pl.when(c == 0)
            def _():
                relay_over_y(part, s).start()

            @pl.when(c == 1)
            def _():
                relay_over_x(part, s).start()

            over_core(part, s, 1).start()
            over_core(part, s, 2).start()

    def gather_third(part):
        for s in others:
            got(eighth(part, s, diagonal), g_r.at[3, part, s])
            over_core(part, s, 3).start()

    def halve(part, j):
        high, low = split(rot_b[part, (z, *others)[j]])
        rot_s[part, 0, j * depth:(j + 1) * depth] = high
        rot_s[part, 1, j * depth:(j + 1) * depth] = low

    def exchange(part):
        for to in others:
            to_band(part, to).start()

    def rotated(part):
        for j, s in enumerate(others):
            for k in range(4):
                got(eighth(part, s, planes[k] + 1 - 2 * c), c_r.at[part, s, k])
            halve(part, j + 1)
        for b in range(0, n, 2):
            columns = slice(b * lanes, (b + 2) * lanes)
            both = jnp.dot(orb_b[...], rot_s[part, 0, :, columns], preferred_element_type=F32)
            cross = jnp.dot(orb_b[:elements * rows], rot_s[part, 1, :, columns], preferred_element_type=F32)
            total = both[:elements * rows] + both[elements * rows:] + cross
            for i in range(elements):
                place = lax.broadcasted_iota(jnp.int32, (rows, 2 * lanes), 0) + z * rows
                piece = jnp.where(place < counts[i], total[i * rows:(i + 1) * rows], F32(0.0))
                res[part, b, i] = piece[:, :lanes]
                res[part, b + 1, i] = piece[:, lanes:]
        if part == 0:
            exchange(part)
        start[part, :, pl.ds(pl.multiple_of(z * rows, rows), rows)] = res[part, z]
        for copy in start_halo(part, z):
            copy.start()

    def spread(part):
        for s in others:
            got(rows_of(start, part, s), a_r.at[part, s])
            for copy in start_halo(part, s):
                copy.start()

    def load(ref, part, i, into, first):
        high, low = split(ref[part, i])
        into[first:first + basis, :lanes] = high
        into[first:first + basis, lanes:] = low

    def fold(r):
        return (r[:basis, :lanes] + r[:basis, lanes:]) + (r[basis:, :lanes] + r[basis:, lanes:])

    def local_slots(ref, part):
        for i in range(-1, elements + 1):
            load(ref, part, i % elements, field_l, (i + 1) * basis)
        for i in range(elements):
            around = field_l[i * basis:(i + 3) * basis]
            acc[part, i] = fold(jnp.dot(ham_l[i], around, preferred_element_type=F32))

    def halo_slots(lo, hi, part, i):
        load(lo, part, i, field_h.at[i], 0)
        load(hi, part, i, field_h.at[i], basis)
        return acc[part, i] + fold(jnp.dot(ham_h[i], field_h[i], preferred_element_type=F32))

    def middle(part):
        for s in range(n):
            got(rows_of(start_lo, part, s), b_r.at[part, s, 0])
            got(rows_of(start_hi, part, s), b_r.at[part, s, 1])
        for i in range(elements):
            mid[part, i] = halo_slots(start_lo, start_hi, part, i)
            for copy in mid_halo(part, i):
                copy.start()

    def finish(part):
        for i in range(elements):
            got(mid_lo.at[part, i], h_r.at[part, i, 0])
            got(mid_hi.at[part, i], h_r.at[part, i, 1])
            total = halo_slots(mid_lo, mid_hi, part, i)
            out[i, :, part * lanes:(part + 1) * lanes] = 2.0 * total - start[part, i]

    def prepare(i):
        square = (basis, basis)
        place = lax.broadcasted_iota(jnp.int32, square, 0)
        scale = jnp.where(place < counts[i], 1.0 / jnp.full(square, width[0], F32), F32(0.0))
        diagonal_part = jnp.where(
            place == lax.broadcasted_iota(jnp.int32, square, 1), center[0], F32(0.0)
        )
        own = (ham_v[i, 0] - diagonal_part) * scale
        for into, blocks in (
            (ham_l, [ham_v[i, 1] * scale, own, ham_v[i, 2] * scale]),
            (ham_h, [ham_v[i, 3] * scale, ham_v[i, 4] * scale]),
        ):
            high, low = split(jnp.concatenate(blocks, axis=1))
            into[i, :basis] = high
            into[i, basis:] = low

    send_own(0)
    orb_copy.wait()
    for j, s in enumerate((z, *others)):
        high, low = split(orb_v[:, pl.ds(pl.multiple_of(s * depth, depth), depth)])
        orb_b[:elements * rows, j * depth:(j + 1) * depth] = high
        orb_b[elements * rows:, j * depth:(j + 1) * depth] = low
    halve(0, 0)
    gather_first(0)
    send_own(1)
    halve(1, 0)
    gather_second(0)
    gather_first(1)
    gather_third(0)
    gather_second(1)
    rotated(0)
    gather_third(1)
    rotated(1)
    spread(0)
    exchange(1)
    ham_copy.wait()
    for i in range(elements):
        prepare(i)
    local_slots(start, 0)
    spread(1)
    middle(0)
    local_slots(start, 1)
    middle(1)
    local_slots(mid, 0)
    finish(0)
    local_slots(mid, 1)
    finish(1)

    for part in range(PARTS):
        for i in range(elements):
            for copy in mid_halo(part, i):
                copy.wait_send()
        for s in range(n):
            for copy in start_halo(part, s):
                copy.wait_send()
        for s in others:
            over_z(part, s).wait_send()
            over_x(part, s).wait_send()
            over_y(part, s).wait_send()
            relay_over_y(part, s).wait_send()
            for k in range(4):
                over_core(part, s, k).wait_send()
            to_band(part, s).wait_send()


def shards(orbitals, rotation, counts, hamiltonian, filter_center, filter_width):
    elements, rows, bands = orbitals.shape
    basis = hamiltonian.shape[2]
    depth = rotation.shape[0]
    n = bands // depth
    lanes = depth // PARTS
    own = (PARTS, elements, basis, lanes)
    dma = pltpu.SemaphoreType.DMA
    in_vmem = pl.BlockSpec(memory_space=pltpu.VMEM)
    in_hbm = pl.BlockSpec(memory_space=pltpu.HBM)
    in_smem = pl.BlockSpec(memory_space=pltpu.SMEM)
    flops = 2 * elements * rows * bands * bands * 3 + 2 * 2 * elements * SLOTS * basis * basis * depth * 4
    return pl.pallas_call(
        functools.partial(kernel, n),
        out_shape=jax.ShapeDtypeStruct((elements, basis, depth), F32),
        in_specs=[in_hbm, in_hbm, in_smem, in_smem, in_smem, in_hbm],
        out_specs=in_vmem,
        scratch_shapes=[
            pltpu.VMEM((elements, SLOTS, basis, basis), F32),
            pltpu.VMEM((elements, 2 * basis, 3 * basis), BF16),
            pltpu.VMEM((elements, 2 * basis, 2 * basis), BF16),
            pltpu.VMEM((elements * rows, bands), F32),
            pltpu.VMEM((2 * elements * rows, bands), BF16),
            pltpu.VMEM((PARTS, n, depth, n * lanes), F32),
            pltpu.VMEM((PARTS, 2, bands, n * lanes), BF16),
            pltpu.VMEM((PARTS, n, elements, rows, lanes), F32),
            pltpu.VMEM(own, F32), pltpu.VMEM(own, F32), pltpu.VMEM(own, F32),
            pltpu.VMEM(own, F32), pltpu.VMEM(own, F32), pltpu.VMEM(own, F32),
            pltpu.VMEM(((elements + 2) * basis, 2 * lanes), BF16),
            pltpu.VMEM((elements, 2 * basis, 2 * lanes), BF16),
            pltpu.VMEM(own, F32),
            dma(()), dma(()), dma((PARTS, n)),
            dma((4, PARTS, n)), dma((4, PARTS, n)),
            dma((PARTS, n, 4)), dma((PARTS, n, 4)),
            dma((PARTS, n)), dma((PARTS, n)),
            dma((PARTS, n, 2)), dma((PARTS, n, 2)),
            dma((PARTS, elements, 2)), dma((PARTS, elements, 2)),
        ],
        compiler_params=pltpu.CompilerParams(
            collective_id=0, has_side_effects=True, vmem_limit_bytes=63 * 1024 * 1024
        ),
        cost_estimate=pl.CostEstimate(flops=flops, bytes_accessed=8 * 1024 * 1024, transcendentals=0),
    )(orbitals.reshape(elements * rows, bands), rotation, counts, filter_center, filter_width, hamiltonian)


def solution(mesh):
    fits = mesh.shape["elem"] == GY and mesh.shape["band"] == 4
    return jax.shard_map(
        shards if fits else general_shards,
        mesh=mesh,
        in_specs=(
            P("elem", "band", None),
            P("band", None),
            P("elem"),
            P("elem", None, None, None),
            P(),
            P(),
        ),
        out_specs=P("elem", None, "band"),
        check_vma=False,
    )
```
